128 devices in a mesh: row: 32 (over y_lo, x, z), col: 4 (over y_hi, core).
Axes of the slice: x: 4, y: 4 (y_hi: 2, y_lo: 2; y = y_hi * 2 + y_lo), z: 4, core: 2. Of those that a mesh axis runs over, the one named last changes fastest.
Arguments:
- old_basis: float32 [12288, 12288], P('row', 'col'), may hold values from -0.0546875 to 0.0546875
- updated_eigen_matrix: float32 [12288, 12288], P('row', 'col'), may hold values from -0.0546875 to 0.0546875
- moment: float32 [12288, 1536], P(('col', 'row')), may hold values from -6 to 6
Outputs:
- moment_in_new_frame: float32 [12288, 1536], P(('col', 'row'))
The draws below stay inside these ranges and needn't reach their ends.
All inputs are finite; a program needn't handle non-finite values.
Results may differ from the reference program's by a relative error of at most 0.00008.
Values sent between devices are 32-bit elements; how exact they have to be, the bound alone decides.
A program may use at most 128 MiB of HBM per device.

```python
import jax
import jax.numpy as jnp
from jax import lax

N = 12288
SLAB = 1536


def steps_of(key, shape, cuts, least, largest):
    factor_of, own = 1.0, jax.random.fold_in(key, 6)
    for dim, shards_of in cuts:
        heights = jnp.exp(jax.random.uniform(jax.random.fold_in(own, dim), (shards_of,), jnp.float32, least / len(cuts), largest / len(cuts)))
        factor_of = factor_of * jnp.repeat(heights, shape[dim] // shards_of).reshape([-1 if axis == dim else 1 for axis in range(len(shape))])
    return factor_of


def centred(own_key, shape, spread, limit, split=(), held_as=jnp.bfloat16):
    entries = spread * jax.random.normal(own_key, shape, jnp.float32)
    if split:
        entries = entries * steps_of(own_key, shape, split, -0.22, 0.18)
    return jnp.clip(entries, -limit, limit).astype(held_as)


def setup_inputs(seed: int = 0) -> dict:
    seeds = jax.random.split(jax.random.key(seed), 4)
    old_basis = centred(seeds[0], (N, N), N ** -0.5, 0.0546875, ((0, 32), (1, 4)), jnp.float32)
    updated_eigen_matrix = centred(seeds[1], (N, N), N ** -0.5, 0.0546875, ((0, 32), (1, 4)), jnp.float32)
    moment = centred(seeds[2], (N, SLAB), 1.0, 6.0, ((0, 128),), jnp.float32)
    return {"old_basis": old_basis, "updated_eigen_matrix": updated_eigen_matrix, "moment": moment}


def reference(old_basis, updated_eigen_matrix, moment):
    standard_frame_moment = jnp.dot(old_basis, moment, preferred_element_type=jnp.float32, precision=lax.Precision.HIGHEST)
    moment_in_new_frame = lax.dot_general(updated_eigen_matrix, standard_frame_moment, (((0,), (0,)), ((), ())), precision=lax.Precision.HIGHEST, preferred_element_type=jnp.float32)
    return moment_in_new_frame
```

```python
import functools

import jax
import jax.numpy as jnp
from jax import lax
from jax.experimental import pallas as pl
from jax.experimental.pallas import tpu as pltpu
from jax.sharding import PartitionSpec as P

ROWS, DEPTH, SLAB, PART = 384, 3072, 1536, 96
PLANE = DEPTH // 2
NCH = 3
CH = SLAB // NCH
HW = CH // 2
SLOTS = 2
MESH = pl.DeviceIdType.MESH
F32, BF16 = jnp.float32, jnp.bfloat16


def split(v):
    hi = v.astype(BF16)
    return hi, (v - hi.astype(F32)).astype(BF16)


def kernel(q_hbm, u_hbm, m_hbm, out, mg, qs, uts, urecv, stage, prod, rd, y1, rf, sf, shl, ob, v1, v2, w1, w2,
           ag_s, ag_r, rs_s, rs_r, ar_s, ar_r, pre_s, pre_r, own_sem, u_s, u_r, st_sem):
    row, col = lax.axis_index("row"), lax.axis_index("col")
    ylo, x, z = row // 16, lax.rem(row // 4, 4), lax.rem(row, 4)
    yhi, core = col // 2, lax.rem(col, 2)

    def plus(v, n):
        return lax.rem(v + n, 4)

    def in_plane(xx, zz):
        return (ylo * 16 + xx * 4 + zz, col)

    xp, xm = in_plane(plus(x, 1), z), in_plane(plus(x, 3), z)
    zp, zm = in_plane(x, plus(z, 1)), in_plane(x, plus(z, 3))
    pair = ((1 - ylo) * 16 + x * 4 + z, col)
    far = (row, (1 - yhi) * 2 + core)
    sib = (row, yhi * 2 + 1 - core)

    first = ((x, xp, xm), (z, zp, zm))
    second = ((z, zp, zm), (x, xp, xm))

    def block(h, a, b):
        xx, zz = (a, b) if h == 0 else (b, a)
        return pl.ds(pl.multiple_of(xx * 384 + zz * 96, 32), PART)

    def remote(src, dst, ss, rs, to):
        return pltpu.make_async_remote_copy(src_ref=src, dst_ref=dst, send_sem=ss, recv_sem=rs, device_id=to, device_id_type=MESH)

    sends = {}

    def send(key, src, dst, ss, rs, to):
        sends[key] = lambda: remote(src, dst, ss, rs, to)
        sends[key]().start()

    def landed(dst, ss, rs):
        remote(dst, dst, ss, rs, pair).wait_recv()

    def sent(key):
        sends.pop(key)().wait_send()

    barrier = pltpu.get_barrier_semaphore()
    for other in (xp, xm, zp, zm, pair, far, sib):
        pl.semaphore_signal(barrier, inc=1, device_id=other, device_id_type=MESH)
    pl.semaphore_wait(barrier, 7)

    own_rows = block(0, x, z)

    def columns(j, h):
        return pl.ds(j * CH + h * HW, HW)

    def own_copy(j, h):
        return pltpu.make_async_copy(m_hbm.at[:, columns(j, h)], mg.at[j, h, ylo, own_rows], own_sem.at[j, h])

    for j in range(NCH):
        for h in range(2):
            own_copy(j, h).start()
            send(("pre", j, h), m_hbm.at[:, columns(j, h)], mg.at[j, h, ylo, own_rows], pre_s.at[j, h], pre_r.at[j, h], pair)
    send(("u",), u_hbm.at[:, pl.ds(pl.multiple_of((1 - ylo) * PLANE, 128), PLANE)], urecv, u_s, u_r, pair)

    def load(i):
        if i < 4:
            src = q_hbm.at[:, pl.ds(i * 768, 768)]
        else:
            src = u_hbm.at[:, pl.ds(pl.multiple_of(ylo * PLANE + (i - 4) * 768, 128), 768)]
        return pltpu.make_async_copy(src, stage.at[i % 2], st_sem.at[i % 2])

    def turn(src, depth0, base):
        @pl.loop(0, 6)
        def _(i):
            at = pl.multiple_of(i * 128, 128)
            hi, lo = split(src[:, pl.ds(at, 128)].T)
            seg, r0 = base // 384 + i // 3, pl.multiple_of(lax.rem(i, 3) * 128, 128)
            uts[seg, pl.ds(r0, 128), pl.ds(depth0, 384)] = hi
            uts[seg, pl.ds(r0 + 384, 128), pl.ds(depth0, 384)] = lo

    def prepare(i):
        load(i).wait()
        if i < 4:
            @pl.loop(0, 24)
            def _(r):
                r0 = pl.multiple_of(r * 16, 16)
                hi, lo = split(stage[i % 2, pl.ds(r0, 16), :])
                qs[pl.ds(r0, 16), pl.ds(i * 768, 768)] = hi
                qs[pl.ds(r0 + 384, 16), pl.ds(i * 768, 768)] = lo
        else:
            turn(stage.at[i % 2], pl.multiple_of(ylo * 384, 128), (i - 4) * 768)
        if i + 2 < 6:
            load(i + 2).start()

    load(0).start()
    load(1).start()

    def prepare_received():
        landed(urecv, u_s, u_r)
        for i in range(2):
            turn(urecv.at[:, pl.ds(i * 768, 768)], pl.multiple_of((1 - ylo) * 384, 128), i * 768)

    def piece(j, h, a, b):
        return mg.at[j, h, :, block(h, a, b)]

    def pass_on(j, h, i, a, b, to):
        ref = piece(j, h, a, b)
        send(("ag", j, h, i), ref, ref, ag_s.at[j, h, i], ag_r.at[j, h, i], to)

    def arrived(j, h, i, a, b):
        landed(piece(j, h, a, b), ag_s.at[j, h, i], ag_r.at[j, h, i])

    def half_piece(j, h, part, a, b):
        return mg.at[j, h, part, block(h, a, b)]

    def ag0(j, h):
        (a, ap, am), (b, bp, bm) = first[h], second[h]
        own_copy(j, h).wait()
        landed(mg.at[j, h, 1 - ylo, own_rows], pre_s.at[j, h], pre_r.at[j, h])
        pass_on(j, h, 0, a, b, ap)
        pass_on(j, h, 1, a, b, am)
        pass_on(j, h, 4, a, b, bp)
        pass_on(j, h, 8, a, b, bm)

    def ag1(j, h):
        (a, ap, am), (b, bp, bm) = first[h], second[h]
        for i, rel, part, to in ((0, 3, 0, ap), (1, 1, 1, am)):
            arrived(j, h, i, plus(a, rel), b)
            ref = half_piece(j, h, part, plus(a, rel), b)
            send(("ag", j, h, 2 + part), ref, ref, ag_s.at[j, h, 2 + part], ag_r.at[j, h, 2 + part], to)
            pass_on(j, h, 4 + rel, plus(a, rel), b, bp)
            pass_on(j, h, 8 + rel, plus(a, rel), b, bm)

    def ag2(j, h):
        (a, ap, am), (b, bp, bm) = first[h], second[h]
        for part in range(2):
            landed(half_piece(j, h, part, plus(a, 2), b), ag_s.at[j, h, 2 + part], ag_r.at[j, h, 2 + part])
        pass_on(j, h, 6, plus(a, 2), b, bp)
        pass_on(j, h, 10, plus(a, 2), b, bm)

    def ag3(j, h, rel):
        (a, ap, am), (b, bp, bm) = first[h], second[h]
        aa = plus(a, rel)
        arrived(j, h, 4 + rel, aa, plus(b, 3))
        if rel < 2:
            pass_on(j, h, 12 + rel, aa, plus(b, 3), bp)
        arrived(j, h, 8 + rel, aa, plus(b, 1))
        if rel >= 2:
            pass_on(j, h, 12 + rel, aa, plus(b, 1), bm)

    def ag4(j, h):
        (a, ap, am), (b, bp, bm) = first[h], second[h]
        for rel in range(4):
            arrived(j, h, 12 + rel, plus(a, rel), plus(b, 2))

    def product1(j):
        @pl.loop(0, 2)
        def _(h):
            prod[j, h] = jnp.zeros((ROWS, HW), F32)

            @pl.loop(0, 4)
            def _(i):
                hi, lo = split(mg[j, h, i // 2, pl.ds(pl.multiple_of(lax.rem(i, 2) * 768, 768), 768), :])
                at = pl.ds(pl.multiple_of(i * 768, 128), 768)
                both = jnp.dot(qs[:, at], hi, preferred_element_type=F32)
                rest = jnp.dot(qs[pl.ds(0, 384), at], lo, preferred_element_type=F32)
                prod[j, h] += both[:ROWS] + (both[ROWS:] + rest)

        send(("ar", j, 0), prod.at[j, :, pl.ds(pl.multiple_of((1 - core) * 192, 192), 192)], rd.at[j], ar_s.at[j, 0], ar_r.at[j, 0], sib)

    def sum1(j):
        landed(rd.at[j], ar_s.at[j, 0], ar_r.at[j, 0])
        y1[j] = prod[j, :, pl.ds(pl.multiple_of(core * 192, 192), 192), :] + rd[j]
        send(("ar", j, 1), y1.at[j], rf.at[j], ar_s.at[j, 1], ar_r.at[j, 1], far)

    def sum2(j):
        landed(rf.at[j], ar_s.at[j, 1], ar_r.at[j, 1])
        sf[j, ylo, core] = y1[j] + rf[j]
        ref = sf.at[j, ylo, core]
        send(("ar", j, 2), ref, ref, ar_s.at[j, 2], ar_r.at[j, 2], pair)
        send(("ar", j, 3), ref, ref, ar_s.at[j, 3], ar_r.at[j, 3], sib)

    def sum3(j):
        ref = sf.at[j, 1 - ylo, core]
        landed(ref, ar_s.at[j, 2], ar_r.at[j, 2])
        send(("ar", j, 4), ref, ref, ar_s.at[j, 4], ar_r.at[j, 4], sib)

    def product2(j):
        landed(sf.at[j, ylo, 1 - core], ar_s.at[j, 3], ar_r.at[j, 3])
        landed(sf.at[j, 1 - ylo, 1 - core], ar_s.at[j, 4], ar_r.at[j, 4])
        slot = j % SLOTS
        if j >= SLOTS:
            for h in range(2):
                for i in range(16):
                    sent(("rs", j - SLOTS, h, i))

        @pl.loop(0, 2)
        def _(h):
            @pl.loop(0, 4)
            def _(i):
                hi, lo = split(sf[j, i // 2, lax.rem(i, 2), h])
                at = pl.ds(pl.multiple_of(i * 192, 192), 192)
                shl[0, at, :] = hi
                shl[1, at, :] = lo

            @pl.loop(0, 4)
            def _(seg):
                both = jnp.dot(uts[seg], shl[0], preferred_element_type=F32)
                rest = jnp.dot(uts[seg, pl.ds(0, 384), :], shl[1], preferred_element_type=F32)
                ob[slot, h, pl.ds(pl.multiple_of(seg * 384, 384), 384), :] = both[:384] + (both[384:] + rest)

    def o(j, h, a, b):
        return ob.at[j % SLOTS, h, block(h, a, b)]

    def rs_send(j, h, i, src, dst, to):
        send(("rs", j, h, i), src, dst, rs_s.at[j, h, i], rs_r.at[j, h, i], to)

    def rs_landed(j, h, i, dst):
        landed(dst, rs_s.at[j, h, i], rs_r.at[j, h, i])

    def rs0(j, h):
        (a, ap, am), (b, bp, bm) = first[h], second[h]
        for rel in (0, 2, 1, 3):
            rs_send(j, h, rel, o(j, h, plus(a, rel), plus(b, 2)), v1.at[j, h, rel], bp if rel < 2 else bm)
        for rel in (2, 0, 3, 1):
            if rel >= 2:
                rs_send(j, h, 4 + rel, o(j, h, plus(a, rel), plus(b, 1)), v2.at[j, h, 0, rel], bp)
            else:
                rs_send(j, h, 8 + rel, o(j, h, plus(a, rel), plus(b, 3)), v2.at[j, h, 1, rel], bm)

    def rs1(j, h):
        (a, ap, am), (b, bp, bm) = first[h], second[h]
        for rel in (0, 2, 1, 3):
            rs_landed(j, h, rel, v1.at[j, h, rel])
            ref = o(j, h, plus(a, rel), plus(b, 1 if rel < 2 else 3))
            ref[...] += v1[j, h, rel]
            if rel < 2:
                rs_send(j, h, 4 + rel, ref, v2.at[j, h, 0, rel], bp)
            else:
                rs_send(j, h, 8 + rel, ref, v2.at[j, h, 1, rel], bm)

    def rs2(j, h):
        (a, ap, am), (b, bp, bm) = first[h], second[h]
        for rel in (2, 1, 3, 0):
            for d in range(2):
                rs_landed(j, h, 4 + 4 * d + rel, v2.at[j, h, d, rel])
            ref = o(j, h, plus(a, rel), b)
            ref[...] += v2[j, h, 0, rel] + v2[j, h, 1, rel]
            if rel == 2:
                rs_send(j, h, 12, ref.at[pl.ds(0, 48)], w1.at[j, h, 0], ap)
                rs_send(j, h, 13, ref.at[pl.ds(48, 48)], w1.at[j, h, 1], am)

    def rs3(j, h):
        (a, ap, am), (b, bp, bm) = first[h], second[h]
        for d, rel, to in ((0, 1, ap), (1, 3, am)):
            rs_landed(j, h, 12 + d, w1.at[j, h, d])
            ref = o(j, h, plus(a, rel), b)
            ref[pl.ds(48 * d, 48), :] += w1[j, h, d]
            rs_send(j, h, 14 + d, ref, w2.at[j, h, d], to)

    def rs4(j, h):
        (a, ap, am), (b, bp, bm) = first[h], second[h]
        for d in range(2):
            rs_landed(j, h, 14 + d, w2.at[j, h, d])
        out[:, columns(j, h)] = o(j, h, a, b)[...] + (w2[j, h, 0] + w2[j, h, 1])

    steps = []

    def at(time, what):
        steps.append((time, len(steps), what))

    period = 94.0 / NCH
    for i in range(4):
        at(1.0 + i * 0.1, functools.partial(prepare, i))
    for i in range(4, 6):
        at(period * 0.6 + i * 0.1, functools.partial(prepare, i))
    at(period + 15.0, prepare_received)
    for j in range(NCH):
        t = period * j
        for h in range(2):
            at(t - 0.25 * period, functools.partial(ag0, j, h))
            at(t + 0.25 * period, functools.partial(ag1, j, h))
            at(t + 0.35 * period, functools.partial(ag3, j, h, 0))
            at(t + 0.50 * period, functools.partial(ag2, j, h))
            at(t + 0.64 * period, functools.partial(ag3, j, h, 1))
            at(t + 0.66 * period, functools.partial(ag3, j, h, 3))
            at(t + 0.80 * period, functools.partial(ag3, j, h, 2))
            at(t + 1.0 * period, functools.partial(ag4, j, h))
        e = t + period
        at(e + 0.5, functools.partial(product1, j))
        at(e + 5.0, functools.partial(sum1, j))
        at(e + 5.0 + 0.25 * period, functools.partial(sum2, j))
        at(e + 6.0 + 0.45 * period, functools.partial(sum3, j))
        e = e + 8.0 + 0.45 * period
        at(e, functools.partial(product2, j))
        for h in range(2):
            at(e + 0.1, functools.partial(rs0, j, h))
            at(e + 0.1 + 0.25 * period, functools.partial(rs1, j, h))
            at(e + 0.1 + 0.60 * period, functools.partial(rs2, j, h))
            at(e + 2.0 + 0.70 * period, functools.partial(rs3, j, h))
            at(e + 4.0 + 0.80 * period, functools.partial(rs4, j, h))
    for _, _, what in sorted(steps, key=lambda s: s[:2]):
        what()
    for key in list(sends):
        sent(key)


def per_device(old_basis, updated_eigen_matrix, moment):
    dma = pltpu.SemaphoreType.DMA
    return pl.pallas_call(
        kernel,
        out_shape=jax.ShapeDtypeStruct((PART, SLAB), F32),
        in_specs=[pl.BlockSpec(memory_space=pl.ANY)] * 3,
        out_specs=pl.BlockSpec(memory_space=pltpu.VMEM),
        scratch_shapes=[
            pltpu.VMEM((NCH, 2, 2, PLANE, HW), F32),
            pltpu.VMEM((2 * ROWS, DEPTH), BF16),
            pltpu.VMEM((4, 768, 768), BF16),
            pltpu.VMEM((ROWS, PLANE), F32),
            pltpu.VMEM((2, ROWS, 768), F32),
            pltpu.VMEM((NCH, 2, ROWS, HW), F32),
            pltpu.VMEM((NCH, 2, 192, HW), F32),
            pltpu.VMEM((NCH, 2, 192, HW), F32),
            pltpu.VMEM((NCH, 2, 192, HW), F32),
            pltpu.VMEM((NCH, 2, 2, 2, 192, HW), F32),
            pltpu.VMEM((2, 768, HW), BF16),
            pltpu.VMEM((SLOTS, 2, PLANE, HW), F32),
            pltpu.VMEM((NCH, 2, 4, PART, HW), F32),
            pltpu.VMEM((NCH, 2, 2, 4, PART, HW), F32),
            pltpu.VMEM((NCH, 2, 2, 48, HW), F32),
            pltpu.VMEM((NCH, 2, 2, PART, HW), F32),
            dma((NCH, 2, 16)), dma((NCH, 2, 16)), dma((NCH, 2, 16)), dma((NCH, 2, 16)),
            dma((NCH, 5)), dma((NCH, 5)), dma((NCH, 2)), dma((NCH, 2)), dma((NCH, 2)), dma(()), dma(()), dma((2,)),
        ],
        compiler_params=pltpu.CompilerParams(collective_id=0, has_side_effects=True, vmem_limit_bytes=63 * 2**20),
        cost_estimate=pl.CostEstimate(flops=21_700_000_000, bytes_accessed=10_000_000, transcendentals=0),
        name="rebase",
    )(old_basis, updated_eigen_matrix, moment)


def solution(mesh):
    placed = (P("row", "col"), P("row", "col"), P(("col", "row"), None))
    return jax.shard_map(
        per_device, mesh=mesh, in_specs=placed, out_specs=P(("col", "row"), None), check_vma=False
    )
```

```python
import jax
import jax.numpy as jnp
from jax import lax
from jax.experimental import pallas as pl
from jax.experimental.pallas import tpu as pltpu
from jax.sharding import PartitionSpec as P

ROWS, DEPTH, SLAB, PART = 384, 3072, 1536, 96
PLANE = DEPTH // 2
WIDTHS = (128, 256, 256, 128)
NCH = len(WIDTHS)
FROM = [2 * sum(WIDTHS[:j]) for j in range(NCH)]
ORDER = (
    ("hop", 0), ("prepare", 0), ("prepare", 1), ("prepare", 2), ("prepare", 3), ("ag0", 0, 0), ("ag0", 0, 1),
    ("hop", 1), ("prepare", 4), ("prepare", 5), ("hop", 2), ("hop", 3), ("ag1", 0, 0), ("ag1", 0, 1), ("exchange", 0),
    ("ag0", 1, 0), ("ag0", 1, 1), ("ag2", 0, 0), ("ag2", 0, 1), ("ag0", 2, 0), ("ag0", 2, 1), ("ag1", 1, 0),
    ("ag1", 1, 1), ("ag3", 0, 1), ("ag3", 0, 0), ("ag1", 2, 0), ("take", 0), ("exchange", 1), ("ag1", 2, 1),
    ("ag2", 1, 0), ("ag0", 3, 0), ("ag2", 1, 1), ("ag0", 3, 1), ("ag4", 0, 1), ("product1", 0, 1), ("ag4", 0, 0),
    ("product1", 0, 0), ("sum1", 0, 1), ("ag2", 2, 0), ("ag2", 2, 1), ("ag1", 3, 0), ("sum1", 0, 0), ("take", 1),
    ("exchange", 2), ("sum2", 0, 1), ("sum2", 0, 0), ("ag3", 1, 0), ("ag3", 1, 1), ("ag1", 3, 1), ("take", 2),
    ("exchange", 3), ("sum3", 0, 1), ("sum3", 0, 0), ("ag3", 2, 1), ("ag2", 3, 0), ("ag3", 2, 0), ("take", 3),
    ("product2", 0, 0), ("rs0", 0, 0), ("product2", 0, 1), ("ag4", 1, 0), ("ag4", 1, 1), ("product1", 1, 0),
    ("product1", 1, 1), ("sum1", 1, 0), ("ag2", 3, 1), ("rs0", 0, 1), ("sum1", 1, 1), ("ag4", 2, 1), ("product1", 2, 1),
    ("ag3", 3, 0), ("sum1", 2, 1), ("sum2", 1, 0), ("ag3", 3, 1), ("sum2", 1, 1), ("ag4", 2, 0), ("product1", 2, 0),
    ("rs1", 0, 0), ("sum2", 2, 1), ("rs1", 0, 1), ("sum1", 2, 0), ("sum3", 1, 0), ("ag4", 3, 1), ("product1", 3, 1),
    ("ag4", 3, 0), ("product1", 3, 0), ("sum1", 3, 1), ("rs2", 0, 1), ("product2", 1, 0), ("sum3", 1, 1),
    ("sum1", 3, 0), ("rs2", 0, 0), ("rs3", 0, 1), ("rs0", 1, 0), ("product2", 1, 1), ("sum3", 2, 1), ("rs3", 0, 0),
    ("rs4", 0, 1), ("rs0", 1, 1), ("product2", 2, 1), ("sum2", 2, 0), ("rs4", 0, 0), ("sum2", 3, 1), ("rs1", 1, 0),
    ("rs0", 2, 1), ("sum2", 3, 0), ("rs1", 1, 1), ("sum3", 2, 0), ("rs2", 1, 0), ("sum3", 3, 1), ("product2", 2, 0),
    ("sum3", 3, 0), ("rs0", 2, 0), ("rs1", 2, 1), ("product2", 3, 1), ("product2", 3, 0), ("rs0", 3, 0), ("rs0", 3, 1),
    ("rs1", 2, 0), ("rs2", 1, 1), ("rs3", 1, 0), ("rs1", 3, 0), ("rs2", 2, 1), ("rs1", 3, 1), ("rs2", 2, 0),
    ("rs4", 1, 0), ("rs3", 1, 1), ("rs2", 3, 1), ("rs2", 3, 0), ("rs3", 2, 0), ("rs3", 2, 1), ("rs4", 1, 1),
    ("rs3", 3, 0), ("rs3", 3, 1), ("rs4", 2, 0), ("rs4", 2, 1), ("rs4", 3, 0), ("rs4", 3, 1),
)
MESH = pl.DeviceIdType.MESH
F32, BF16 = jnp.float32, jnp.bfloat16


def split(v):
    hi = v.astype(BF16)
    return hi, (v - hi.astype(F32)).astype(BF16)


def kernel(q_hbm, u_hbm, m_hbm, out, *scratch):
    per_chunk, common = scratch[: 9 * NCH], scratch[9 * NCH :]
    mg, prod, rd, y1, rf, sf, v, w1, w2 = [per_chunk[i * NCH : (i + 1) * NCH] for i in range(9)]
    qs, uts, urecv, stage, shl, ag_s, ag_r, rs_s, rs_r, ar_s, ar_r, pre_s, pre_r, own_sem, u_s, u_r, st_sem = common
    row, col = lax.axis_index("row"), lax.axis_index("col")
    ylo, x, z = row // 16, lax.rem(row // 4, 4), lax.rem(row, 4)
    yhi, core = col // 2, lax.rem(col, 2)

    def plus(v, n):
        return lax.rem(v + n, 4)

    def in_plane(xx, zz):
        return (ylo * 16 + xx * 4 + zz, col)

    xp, xm = in_plane(plus(x, 1), z), in_plane(plus(x, 3), z)
    zp, zm = in_plane(x, plus(z, 1)), in_plane(x, plus(z, 3))
    pair = ((1 - ylo) * 16 + x * 4 + z, col)
    far = (row, (1 - yhi) * 2 + core)
    sib = (row, yhi * 2 + 1 - core)

    first = ((x, xp, xm), (z, zp, zm))
    second = ((z, zp, zm), (x, xp, xm))

    def remote(src, dst, ss, rs, to):
        return pltpu.make_async_remote_copy(src_ref=src, dst_ref=dst, send_sem=ss, recv_sem=rs, device_id=to, device_id_type=MESH)

    sends = {}

    pairs = {"ag": (ag_s, ag_r), "rs": (rs_s, rs_r), "ar": (ar_s, ar_r), "pre": (pre_s, pre_r), "u": (u_s, u_r)}

    def copy(key, src, dst, to):
        ss, rs = (sem.at[key[1:]] for sem in pairs[key[0]])
        return remote(src, dst, ss, rs, to)

    def send(key, src, dst, to):
        sends[key] = lambda: copy(key, src, dst, to)
        sends[key]().start()

    def landed(key, dst):
        copy(key, dst, dst, pair).wait_recv()

    def sent(key):
        sends.pop(key)().wait_send()

    barrier = pltpu.get_barrier_semaphore()
    for other in (xp, xm, zp, zm, pair, far, sib):
        pl.semaphore_signal(barrier, inc=1, device_id=other, device_id_type=MESH)
    pl.semaphore_wait(barrier, 7)

    def columns(j, h):
        return pl.ds(FROM[j] + h * WIDTHS[j], WIDTHS[j])

    def own_copy(j, h):
        return pltpu.make_async_copy(m_hbm.at[:, columns(j, h)], mg[j].at[h, ylo, x, z], own_sem.at[j, h])

    def hop(j):
        for h in range(2):
            own_copy(j, h).start()
            send(("pre", j, h), m_hbm.at[:, columns(j, h)], mg[j].at[h, ylo, x, z], pair)

    def exchange(i):
        at = pl.multiple_of((1 - ylo) * PLANE + 384 * i, 128)
        send(("u", i), u_hbm.at[:, pl.ds(at, 384)], urecv.at[i], pair)

    def load(i):
        if i < 4:
            src = q_hbm.at[:, pl.ds(i * 768, 768)]
        else:
            src = u_hbm.at[:, pl.ds(pl.multiple_of(ylo * PLANE + (i - 4) * 768, 128), 768)]
        return pltpu.make_async_copy(src, stage.at[i % 2], st_sem.at[i % 2])

    def turn(src, seg, depth0):
        @pl.loop(0, 3)
        def _(i):
            at = pl.multiple_of(i * 128, 128)
            hi, lo = split(src[:, pl.ds(at, 128)].T)
            uts[seg, pl.ds(at, 128), pl.ds(depth0, 384)] = hi
            uts[seg, pl.ds(at + 384, 128), pl.ds(depth0, 384)] = lo

    def prepare(i):
        load(i).wait()
        if i < 4:
            @pl.loop(0, 12)
            def _(r):
                r0 = pl.multiple_of(r * 32, 32)
                hi, lo = split(stage[i % 2, pl.ds(r0, 32), :])
                qs[pl.ds(r0, 32), pl.ds(i * 768, 768)] = hi
                qs[pl.ds(r0 + 384, 32), pl.ds(i * 768, 768)] = lo
        else:
            for half in range(2):
                turn(stage.at[i % 2, :, pl.ds(384 * half, 384)], 2 * (i - 4) + half, pl.multiple_of(ylo * 384, 128))
        if i + 2 < 6:
            load(i + 2).start()

    load(0).start()
    load(1).start()

    def take(i):
        landed(("u", i), urecv.at[i])
        turn(urecv.at[i], i, pl.multiple_of((1 - ylo) * 384, 128))

    def piece(j, h, a, b):
        return mg[j].at[h, :, a, b] if h == 0 else mg[j].at[h, :, b, a]

    def line(j, h, part, b):
        return mg[j].at[h, part, :, b] if h == 0 else mg[j].at[h, part, b]

    def lines(j, h, b):
        return mg[j].at[h, :, :, b] if h == 0 else mg[j].at[h, :, b]

    def half_piece(j, h, part, a, b):
        return mg[j].at[h, part, a, b] if h == 0 else mg[j].at[h, part, b, a]

    def pass_on(j, h, i, ref, to):
        send(("ag", j, h, i), ref, ref, to)

    def arrived(j, h, i, ref):
        landed(("ag", j, h, i), ref)

    def ag0(j, h):
        (a, ap, am), (b, bp, bm) = first[h], second[h]
        own_copy(j, h).wait()
        landed(("pre", j, h), mg[j].at[h, 1 - ylo, x, z])
        pass_on(j, h, 0, piece(j, h, a, b), ap)
        pass_on(j, h, 1, piece(j, h, a, b), am)

    def ag1(j, h):
        (a, ap, am), (b, bp, bm) = first[h], second[h]
        for i, rel, to in ((0, 3, ap), (1, 1, am)):
            arrived(j, h, i, piece(j, h, plus(a, rel), b))
            pass_on(j, h, 2 + i, half_piece(j, h, i, plus(a, rel), b), to)

    def ag2(j, h):
        (a, ap, am), (b, bp, bm) = first[h], second[h]
        for i in range(2):
            arrived(j, h, 2 + i, half_piece(j, h, i, plus(a, 2), b))
        pass_on(j, h, 4, lines(j, h, b), bp)
        pass_on(j, h, 5, lines(j, h, b), bm)

    def ag3(j, h):
        (a, ap, am), (b, bp, bm) = first[h], second[h]
        for i, rel, to in ((0, 3, bp), (1, 1, bm)):
            arrived(j, h, 4 + i, lines(j, h, plus(b, rel)))
            pass_on(j, h, 6 + i, line(j, h, i, plus(b, rel)), to)

    def ag4(j, h):
        (a, ap, am), (b, bp, bm) = first[h], second[h]
        for i in range(2):
            arrived(j, h, 6 + i, line(j, h, i, plus(b, 2)))

    def ar_send(j, h, i, src, dst, to):
        send(("ar", j, h, i), src, dst, to)

    def ar_landed(j, h, i, dst):
        landed(("ar", j, h, i), dst)

    def product1(j, h):
        prod[j][h] = jnp.zeros((ROWS, WIDTHS[j]), F32)

        @pl.loop(0, 4)
        def _(i):
            hi, lo = split(mg[j][h, i // 2, pl.ds(lax.rem(i, 2) * 2, 2)].reshape(768, WIDTHS[j]))
            at = pl.ds(pl.multiple_of(i * 768, 128), 768)
            both = jnp.dot(qs[:, at], hi, preferred_element_type=F32)
            rest = jnp.dot(qs[pl.ds(0, 384), at], lo, preferred_element_type=F32)
            prod[j][h] += both[:ROWS] + (both[ROWS:] + rest)

        ar_send(j, h, 0, prod[j].at[h, pl.ds(pl.multiple_of((1 - core) * 192, 192), 192)], rd[j].at[h], sib)

    def sum1(j, h):
        ar_landed(j, h, 0, rd[j].at[h])
        y1[j][h] = prod[j][h, pl.ds(pl.multiple_of(core * 192, 192), 192), :] + rd[j][h]
        ar_send(j, h, 1, y1[j].at[h], rf[j].at[h], far)

    def sum2(j, h):
        ar_landed(j, h, 1, rf[j].at[h])
        sf[j][h, ylo, core] = y1[j][h] + rf[j][h]
        ref = sf[j].at[h, ylo, core]
        ar_send(j, h, 2, ref, ref, pair)
        ar_send(j, h, 3, ref, ref, sib)

    def sum3(j, h):
        ref = sf[j].at[h, 1 - ylo, core]
        ar_landed(j, h, 2, ref)
        ar_send(j, h, 4, ref, ref, sib)

    def product2(j, h):
        w = WIDTHS[j]
        ar_landed(j, h, 3, sf[j].at[h, ylo, 1 - core])
        ar_landed(j, h, 4, sf[j].at[h, 1 - ylo, 1 - core])
        for i in range(8):
            sent(("ag", j, h, i))

        @pl.loop(0, 4)
        def _(i):
            hi, lo = split(sf[j][h, i // 2, lax.rem(i, 2)])
            at = pl.ds(pl.multiple_of(i * 192, 192), 192)
            shl[0, at, pl.ds(0, w)] = hi
            shl[1, at, pl.ds(0, w)] = lo

        @pl.loop(0, 4)
        def _(seg):
            both = jnp.dot(uts[seg], shl[0, :, pl.ds(0, w)], preferred_element_type=F32)
            rest = jnp.dot(uts[seg, pl.ds(0, 384), :], shl[1, :, pl.ds(0, w)], preferred_element_type=F32)
            mg[j][h, 0, seg] = (both[:384] + (both[384:] + rest)).reshape(4, PART, w)

    def o(j, h, a, b):
        return half_piece(j, h, 0, a, b)

    def rs_send(j, h, i, src, dst, to):
        send(("rs", j, h, i), src, dst, to)

    def rs_landed(j, h, i, dst):
        landed(("rs", j, h, i), dst)

    def rs0(j, h):
        (a, ap, am), (b, bp, bm) = first[h], second[h]
        for rel in (0, 2, 1, 3):
            rs_send(j, h, rel, o(j, h, plus(a, rel), plus(b, 2)), v[j].at[h, 0, rel], bp if rel < 2 else bm)
        for rel in (2, 0, 3, 1):
            if rel >= 2:
                rs_send(j, h, 4 + rel, o(j, h, plus(a, rel), plus(b, 1)), v[j].at[h, 1, rel], bp)
            else:
                rs_send(j, h, 8 + rel, o(j, h, plus(a, rel), plus(b, 3)), v[j].at[h, 2, rel], bm)

    def rs1(j, h):
        (a, ap, am), (b, bp, bm) = first[h], second[h]
        for rel in (0, 2, 1, 3):
            rs_landed(j, h, rel, v[j].at[h, 0, rel])
            ref = o(j, h, plus(a, rel), plus(b, 1 if rel < 2 else 3))
            ref[...] += v[j][h, 0, rel]
            if rel < 2:
                rs_send(j, h, 4 + rel, ref, v[j].at[h, 1, rel], bp)
            else:
                rs_send(j, h, 8 + rel, ref, v[j].at[h, 2, rel], bm)

    def rs2(j, h):
        (a, ap, am), (b, bp, bm) = first[h], second[h]
        for rel in (2, 1, 3, 0):
            for d in range(2):
                rs_landed(j, h, 4 + 4 * d + rel, v[j].at[h, 1 + d, rel])
            ref = o(j, h, plus(a, rel), b)
            ref[...] += v[j][h, 1, rel] + v[j][h, 2, rel]
            if rel == 2:
                rs_send(j, h, 12, ref.at[pl.ds(0, 48)], w1[j].at[h, 0], ap)
                rs_send(j, h, 13, ref.at[pl.ds(48, 48)], w1[j].at[h, 1], am)

    def rs3(j, h):
        (a, ap, am), (b, bp, bm) = first[h], second[h]
        for d, rel, to in ((0, 1, ap), (1, 3, am)):
            rs_landed(j, h, 12 + d, w1[j].at[h, d])
            ref = o(j, h, plus(a, rel), b)
            ref[pl.ds(48 * d, 48), :] += w1[j][h, d]
            rs_send(j, h, 14 + d, ref, w2[j].at[h, d], to)

    def rs4(j, h):
        (a, ap, am), (b, bp, bm) = first[h], second[h]
        for d in range(2):
            rs_landed(j, h, 14 + d, w2[j].at[h, d])
        out[:, columns(j, h)] = o(j, h, a, b)[...] + (w2[j][h, 0] + w2[j][h, 1])

    steps = dict(
        hop=hop, prepare=prepare, exchange=exchange, take=take, ag0=ag0, ag1=ag1, ag2=ag2, ag3=ag3, ag4=ag4,
        product1=product1, sum1=sum1, sum2=sum2, sum3=sum3, product2=product2, rs0=rs0, rs1=rs1, rs2=rs2, rs3=rs3, rs4=rs4,
    )
    for name, *where in ORDER:
        steps[name](*where)
    for key in list(sends):
        sent(key)


def per_device(old_basis, updated_eigen_matrix, moment):
    dma = pltpu.SemaphoreType.DMA
    shapes = ((2, 4, 4, PART), (ROWS,), (192,), (192,), (192,), (2, 2, 192), (3, 4, PART), (2, 48), (2, PART))
    return pl.pallas_call(
        kernel,
        out_shape=jax.ShapeDtypeStruct((PART, SLAB), F32),
        in_specs=[pl.BlockSpec(memory_space=pl.ANY)] * 3,
        out_specs=pl.BlockSpec(memory_space=pltpu.VMEM),
        scratch_shapes=[pltpu.VMEM((2, *shape, w), F32) for shape in shapes for w in WIDTHS] + [
            pltpu.VMEM((2 * ROWS, DEPTH), BF16),
            pltpu.VMEM((4, 768, 768), BF16),
            pltpu.VMEM((4, ROWS, 384), F32),
            pltpu.VMEM((2, ROWS, 768), F32),
            pltpu.VMEM((2, 768, max(WIDTHS)), BF16),
            dma((NCH, 2, 8)), dma((NCH, 2, 8)), dma((NCH, 2, 16)), dma((NCH, 2, 16)),
            dma((NCH, 2, 5)), dma((NCH, 2, 5)), dma((NCH, 2)), dma((NCH, 2)), dma((NCH, 2)), dma((4,)), dma((4,)), dma((2,)),
        ],
        compiler_params=pltpu.CompilerParams(collective_id=0, has_side_effects=True, vmem_limit_bytes=63 * 2**20),
        cost_estimate=pl.CostEstimate(flops=21_700_000_000, bytes_accessed=10_000_000, transcendentals=0),
        name="rebase",
    )(old_basis, updated_eigen_matrix, moment)


def solution(mesh):
    placed = (P("row", "col"), P("row", "col"), P(("col", "row"), None))
    return jax.shard_map(
        per_device, mesh=mesh, in_specs=placed, out_specs=P(("col", "row"), None), check_vma=False
    )
```

```python
import jax
import jax.numpy as jnp
from jax import lax
from jax.experimental import pallas as pl
from jax.experimental.pallas import tpu as pltpu
from jax.sharding import PartitionSpec as P

ROWS, DEPTH, SLAB, PART = 384, 3072, 1536, 96
PLANE = DEPTH // 2
WIDTHS = (256, 128, 128, 128, 128)
NCH = len(WIDTHS)
FROM = [2 * sum(WIDTHS[:j]) for j in range(NCH)]
ORDER = (
    ("hop", 0), ("ag0", 0, 0), ("ag0", 0, 1), ("ag0", 1, 0), ("ag0", 1, 1), ("prepare", 0), ("prepare", 1),
    ("prepare", 2), ("prepare", 3), ("agx", 0, 0), ("agx", 0, 1), ("hop", 1), ("prepare", 4), ("prepare", 5),
    ("hop", 2), ("ag0", 2, 0), ("ag0", 2, 1), ("hop", 3), ("ag0", 3, 0), ("ag0", 3, 1), ("hop", 4), ("agx", 1, 0),
    ("ag1", 0, 0), ("ag1", 0, 1), ("agx", 1, 1), ("agx", 2, 0), ("agx", 2, 1), ("ag1", 1, 0), ("agx", 3, 0),
    ("ag2", 0, 1), ("agx", 3, 1), ("ag0", 4, 1), ("ag2", 0, 0), ("ag1", 1, 1), ("exchange", 0), ("exchange", 1),
    ("exchange", 2), ("exchange", 3), ("ag0", 4, 0), ("ag1", 2, 0), ("ag1", 2, 1), ("agx", 4, 0), ("agx", 4, 1),
    ("ag2", 1, 0), ("ag1", 3, 1), ("ag1", 3, 0), ("ag3", 0, 1), ("ag3", 0, 0), ("ag2", 1, 1), ("ag2", 2, 0),
    ("ag2", 2, 1), ("ag1", 4, 0), ("ag1", 4, 1), ("ag2", 3, 0), ("ag3", 1, 0), ("ag4", 0, 1), ("product1", 0, 1),
    ("ag2", 3, 1), ("sum1", 0, 1), ("ag3", 1, 1), ("ag4", 0, 0), ("product1", 0, 0), ("sum1", 0, 0), ("ag3", 2, 1),
    ("ag3", 2, 0), ("ag2", 4, 0), ("ag2", 4, 1), ("take", 0), ("take", 1), ("take", 2), ("take", 3), ("sum2", 0, 1),
    ("ag3", 3, 1), ("ag3", 3, 0), ("sum2", 0, 0), ("ag4", 1, 1), ("ag4", 1, 0), ("product1", 1, 0), ("sum3", 0, 1),
    ("ag4", 2, 1), ("ag4", 2, 0), ("sum1", 1, 0), ("product1", 2, 0), ("sum3", 0, 0), ("product2", 0, 1),
    ("sum1", 2, 0), ("product2", 0, 0), ("sum2", 1, 0), ("ag3", 4, 0), ("ag3", 4, 1), ("rs0", 0, 0), ("rs0", 0, 1),
    ("ag4", 3, 1), ("ag4", 3, 0), ("sum2", 2, 0), ("product1", 3, 0), ("sum3", 1, 0), ("ag4", 4, 1), ("ag4", 4, 0),
    ("product1", 4, 0), ("sum1", 3, 0), ("product2", 1, 0), ("sum3", 2, 0), ("sum1", 4, 0), ("rs1", 0, 0),
    ("rs1", 0, 1), ("rs0", 1, 0), ("rs0", 1, 1), ("product2", 2, 0), ("sum2", 3, 0), ("rs0", 2, 0), ("rs0", 2, 1),
    ("rs2", 0, 0), ("rs2", 0, 1), ("sum2", 4, 0), ("rs1", 1, 0), ("rs1", 1, 1), ("sum3", 3, 0), ("rs1", 2, 0),
    ("rs1", 2, 1), ("product2", 3, 0), ("sum3", 4, 0), ("rs3", 0, 0), ("rs3", 0, 1), ("rs0", 3, 0), ("rs0", 3, 1),
    ("rs2", 1, 0), ("rs2", 1, 1), ("product2", 4, 0), ("rs2", 2, 0), ("rs2", 2, 1), ("rs4", 0, 1), ("rs4", 0, 0),
    ("rs0", 4, 0), ("rs0", 4, 1), ("rs1", 3, 0), ("rs1", 3, 1), ("rs3", 1, 1), ("rs3", 1, 0), ("rs3", 2, 1),
    ("rs3", 2, 0), ("rs1", 4, 0), ("rs1", 4, 1), ("rs2", 3, 0), ("rs2", 3, 1), ("rs4", 1, 1), ("rs4", 1, 0),
    ("rs4", 2, 1), ("rs4", 2, 0), ("rs2", 4, 0), ("rs2", 4, 1), ("rs3", 3, 0), ("rs3", 3, 1), ("rs3", 4, 0),
    ("rs3", 4, 1), ("rs4", 3, 0), ("rs4", 3, 1), ("rs4", 4, 0), ("rs4", 4, 1),
)
MESH = pl.DeviceIdType.MESH
F32, BF16 = jnp.float32, jnp.bfloat16


def split(v):
    hi = v.astype(BF16)
    return hi, (v - hi.astype(F32)).astype(BF16)


def kernel(q_hbm, u_hbm, m_hbm, out, *scratch):
    per_chunk, common = scratch[: 9 * NCH], scratch[9 * NCH :]
    mg, prod, rd, y1, rf, sf, v, w1, w2 = [per_chunk[i * NCH : (i + 1) * NCH] for i in range(9)]
    qs, uts, urecv, stage, shl, ag_s, ag_r, rs_s, rs_r, ar_s, ar_r, pre_s, pre_r, own_sem, u_s, u_r, st_sem = common
    row, col = lax.axis_index("row"), lax.axis_index("col")
    ylo, x, z = row // 16, lax.rem(row // 4, 4), lax.rem(row, 4)
    yhi, core = col // 2, lax.rem(col, 2)

    def plus(v, n):
        return lax.rem(v + n, 4)

    def in_plane(xx, zz):
        return (ylo * 16 + xx * 4 + zz, col)

    xp, xm = in_plane(plus(x, 1), z), in_plane(plus(x, 3), z)
    zp, zm = in_plane(x, plus(z, 1)), in_plane(x, plus(z, 3))
    pair = ((1 - ylo) * 16 + x * 4 + z, col)
    far = (row, (1 - yhi) * 2 + core)
    sib = (row, yhi * 2 + 1 - core)

    first = ((x, xp, xm), (z, zp, zm))
    second = ((z, zp, zm), (x, xp, xm))

    def remote(src, dst, ss, rs, to):
        return pltpu.make_async_remote_copy(src_ref=src, dst_ref=dst, send_sem=ss, recv_sem=rs, device_id=to, device_id_type=MESH)

    sends = {}

    pairs = {"ag": (ag_s, ag_r), "rs": (rs_s, rs_r), "ar": (ar_s, ar_r), "pre": (pre_s, pre_r), "u": (u_s, u_r)}

    def copy(key, src, dst, to):
        ss, rs = (sem.at[key[1:]] for sem in pairs[key[0]])
        return remote(src, dst, ss, rs, to)

    def send(key, src, dst, to):
        sends[key] = lambda: copy(key, src, dst, to)
        sends[key]().start()

    def landed(key, dst):
        copy(key, dst, dst, pair).wait_recv()

    def sent(key):
        sends.pop(key)().wait_send()

    barrier = pltpu.get_barrier_semaphore()
    for other in (xp, xm, zp, zm, pair, far, sib):
        pl.semaphore_signal(barrier, inc=1, device_id=other, device_id_type=MESH)
    pl.semaphore_wait(barrier, 7)

    def columns(j, h):
        return pl.ds(FROM[j] + h * WIDTHS[j], WIDTHS[j])

    def own_piece(j, h, part):
        return mg[j].at[h, part, z, x] if h == 0 else mg[j].at[h, part, x, z]

    def own_copy(j, h):
        return pltpu.make_async_copy(m_hbm.at[:, columns(j, h)], own_piece(j, h, ylo), own_sem.at[j, h])

    def hop(j):
        for h in range(2):
            send(("pre", j, h), m_hbm.at[:, columns(j, h)], own_piece(j, h, ylo), pair)

    for j in range(NCH):
        for h in range(2):
            own_copy(j, h).start()

    def exchange(i):
        at = pl.multiple_of((1 - ylo) * PLANE + 384 * i, 128)
        send(("u", i), u_hbm.at[:, pl.ds(at, 384)], urecv.at[i], pair)

    def load(i):
        if i < 4:
            src = q_hbm.at[:, pl.ds(i * 768, 768)]
        else:
            src = u_hbm.at[:, pl.ds(pl.multiple_of(ylo * PLANE + (i - 4) * 768, 128), 768)]
        return pltpu.make_async_copy(src, stage.at[i % 2], st_sem.at[i % 2])

    def turn(src, seg, depth0):
        @pl.loop(0, 3)
        def _(i):
            at = pl.multiple_of(i * 128, 128)
            hi, lo = split(src[:, pl.ds(at, 128)].T)
            uts[seg, pl.ds(at, 128), pl.ds(depth0, 384)] = hi
            uts[seg, pl.ds(at + 384, 128), pl.ds(depth0, 384)] = lo

    def prepare(i):
        load(i).wait()
        if i < 4:
            @pl.loop(0, 12)
            def _(r):
                r0 = pl.multiple_of(r * 32, 32)
                hi, lo = split(stage[i % 2, pl.ds(r0, 32), :])
                qs[pl.ds(r0, 32), pl.ds(i * 768, 768)] = hi
                qs[pl.ds(r0 + 384, 32), pl.ds(i * 768, 768)] = lo
        else:
            for half in range(2):
                turn(stage.at[i % 2, :, pl.ds(384 * half, 384)], 2 * (i - 4) + half, pl.multiple_of(ylo * 384, 128))
        if i + 2 < 6:
            load(i + 2).start()

    load(0).start()
    load(1).start()

    def take(i):
        landed(("u", i), urecv.at[i])
        turn(urecv.at[i], i, pl.multiple_of((1 - ylo) * 384, 128))

    def piece(j, h, a, b):
        return mg[j].at[h, :, b, a]

    def line(j, h, part, b):
        return mg[j].at[h, part, b]

    def lines(j, h, b):
        return mg[j].at[h, :, b]

    def half_piece(j, h, part, a, b):
        return mg[j].at[h, part, b, a]

    def pass_on(j, h, i, ref, to):
        send(("ag", j, h, i), ref, ref, to)

    def arrived(j, h, i, ref):
        landed(("ag", j, h, i), ref)

    def ag0(j, h):
        (a, ap, am), (b, bp, bm) = first[h], second[h]
        own_copy(j, h).wait()
        pass_on(j, h, 0, half_piece(j, h, ylo, a, b), ap)
        pass_on(j, h, 1, half_piece(j, h, ylo, a, b), am)

    def agx(j, h):
        (a, ap, am), (b, bp, bm) = first[h], second[h]
        landed(("pre", j, h), own_piece(j, h, 1 - ylo))
        pass_on(j, h, 8, half_piece(j, h, 1 - ylo, a, b), ap)
        pass_on(j, h, 9, half_piece(j, h, 1 - ylo, a, b), am)

    def ag1(j, h):
        (a, ap, am), (b, bp, bm) = first[h], second[h]
        for i, rel, to in ((0, 3, ap), (1, 1, am)):
            arrived(j, h, i, half_piece(j, h, ylo, plus(a, rel), b))
            arrived(j, h, 8 + i, half_piece(j, h, 1 - ylo, plus(a, rel), b))
            pass_on(j, h, 2 + i, half_piece(j, h, i, plus(a, rel), b), to)

    def ag2(j, h):
        (a, ap, am), (b, bp, bm) = first[h], second[h]
        for i in range(2):
            arrived(j, h, 2 + i, half_piece(j, h, i, plus(a, 2), b))
        pass_on(j, h, 4, lines(j, h, b), bp)
        pass_on(j, h, 5, lines(j, h, b), bm)

    def ag3(j, h):
        (a, ap, am), (b, bp, bm) = first[h], second[h]
        for i, rel, to in ((0, 3, bp), (1, 1, bm)):
            arrived(j, h, 4 + i, lines(j, h, plus(b, rel)))
            pass_on(j, h, 6 + i, line(j, h, i, plus(b, rel)), to)

    def ag4(j, h):
        (a, ap, am), (b, bp, bm) = first[h], second[h]
        for i in range(2):
            arrived(j, h, 6 + i, line(j, h, i, plus(b, 2)))

    def halves(j, g):
        return ((0, 1), pl.ds(0, 2)) if WIDTHS[j] < 256 else ((g,), pl.ds(g, 1))

    def ar_send(j, g, i, src, dst, to):
        send(("ar", j, g, i), src, dst, to)

    def ar_landed(j, g, i, dst):
        landed(("ar", j, g, i), dst)

    def moment_rows(j, h, part, x0):
        if h == 0:
            return jnp.concatenate([mg[j][0, part, zz, x0 + xx] for xx in range(2) for zz in range(4)], axis=0)
        return mg[j][1, part, pl.ds(x0, 2)].reshape(768, WIDTHS[j])

    def product1(j, g):
        hs, sl = halves(j, g)
        w = WIDTHS[j]
        prod[j][sl] = jnp.zeros((len(hs), ROWS, w), F32)

        @pl.loop(0, 4)
        def _(i):
            rows = [moment_rows(j, h, i // 2, lax.rem(i, 2) * 2) for h in hs]
            hi, lo = split(jnp.concatenate(rows, axis=1) if len(hs) > 1 else rows[0])
            at = pl.ds(pl.multiple_of(i * 768, 128), 768)
            both = jnp.dot(qs[:, at], hi, preferred_element_type=F32)
            rest = jnp.dot(qs[pl.ds(0, 384), at], lo, preferred_element_type=F32)
            total = both[:ROWS] + (both[ROWS:] + rest)
            for n, h in enumerate(hs):
                prod[j][h] += total[:, n * w : (n + 1) * w]

        ar_send(j, g, 0, prod[j].at[sl, pl.ds(pl.multiple_of((1 - core) * 192, 192), 192)], rd[j].at[sl], sib)

    def sum1(j, g):
        hs, sl = halves(j, g)
        ar_landed(j, g, 0, rd[j].at[sl])
        y1[j][sl] = prod[j][sl, pl.ds(pl.multiple_of(core * 192, 192), 192), :] + rd[j][sl]
        ar_send(j, g, 1, y1[j].at[sl], rf[j].at[sl], far)

    def sum2(j, g):
        hs, sl = halves(j, g)
        ar_landed(j, g, 1, rf[j].at[sl])
        sf[j][sl, ylo, core] = y1[j][sl] + rf[j][sl]
        ref = sf[j].at[sl, ylo, core]
        ar_send(j, g, 2, ref, ref, pair)
        ar_send(j, g, 3, ref, ref, sib)

    def sum3(j, g):
        hs, sl = halves(j, g)
        ref = sf[j].at[sl, 1 - ylo, core]
        ar_landed(j, g, 2, ref)
        ar_send(j, g, 4, ref, ref, sib)

    def product2(j, g):
        hs, sl = halves(j, g)
        w = WIDTHS[j]
        ar_landed(j, g, 3, sf[j].at[sl, ylo, 1 - core])
        ar_landed(j, g, 4, sf[j].at[sl, 1 - ylo, 1 - core])
        for h in hs:
            for i in range(10):
                sent(("ag", j, h, i))

        @pl.loop(0, 4)
        def _(i):
            at = pl.ds(pl.multiple_of(i * 192, 192), 192)
            for n, h in enumerate(hs):
                hi, lo = split(sf[j][h, i // 2, lax.rem(i, 2)])
                shl[0, at, pl.ds(n * w, w)] = hi
                shl[1, at, pl.ds(n * w, w)] = lo

        @pl.loop(0, 4)
        def _(seg):
            both = jnp.dot(uts[seg], shl[0, :, pl.ds(0, len(hs) * w)], preferred_element_type=F32)
            rest = jnp.dot(uts[seg, pl.ds(0, 384), :], shl[1, :, pl.ds(0, len(hs) * w)], preferred_element_type=F32)
            total = both[:384] + (both[384:] + rest)
            for n, h in enumerate(hs):
                blocks = total[:, n * w : (n + 1) * w].reshape(4, PART, w)
                if h == 0:
                    mg[j][0, 0, :, seg] = blocks
                else:
                    mg[j][1, 0, seg] = blocks

    def o(j, h, a, b):
        return mg[j].at[h, 0, b, a]

    def half(k):
        return pl.ds(2 * k, 2)

    def o_half(j, h, k, b):
        return mg[j].at[h, 0, b, half(k)]

    def rs_send(j, h, i, src, dst, to):
        send(("rs", j, h, i), src, dst, to)

    def rs_landed(j, h, i, dst):
        landed(("rs", j, h, i), dst)

    def rs0(j, h):
        (a, ap, am), (b, bp, bm) = first[h], second[h]
        rs_send(j, h, 0, o_half(j, h, 0, plus(b, 2)), v[j].at[h, 0, half(0)], bp)
        rs_send(j, h, 1, o_half(j, h, 1, plus(b, 2)), v[j].at[h, 0, half(1)], bm)
        rs_send(j, h, 2, o_half(j, h, 1, plus(b, 1)), v[j].at[h, 1, half(1)], bp)
        rs_send(j, h, 3, o_half(j, h, 0, plus(b, 3)), v[j].at[h, 2, half(0)], bm)

    def rs1(j, h):
        (a, ap, am), (b, bp, bm) = first[h], second[h]
        for k, bb, to in ((0, plus(b, 1), bp), (1, plus(b, 3), bm)):
            rs_landed(j, h, k, v[j].at[h, 0, half(k)])
            ref = o_half(j, h, k, bb)
            ref[...] += v[j][h, 0, half(k)]
            rs_send(j, h, 4 + k, ref, v[j].at[h, 1 + k, half(k)], to)

    def rs2(j, h):
        (a, ap, am), (b, bp, bm) = first[h], second[h]
        rs_landed(j, h, 2, v[j].at[h, 1, half(1)])
        rs_landed(j, h, 3, v[j].at[h, 2, half(0)])
        rs_landed(j, h, 4, v[j].at[h, 1, half(0)])
        rs_landed(j, h, 5, v[j].at[h, 2, half(1)])
        ref = mg[j].at[h, 0, b]
        ref[...] += v[j][h, 1] + v[j][h, 2]
        far_block = o(j, h, plus(a, 2), b)
        rs_send(j, h, 6, far_block.at[pl.ds(0, 48)], w1[j].at[h, 0], ap)
        rs_send(j, h, 7, far_block.at[pl.ds(48, 48)], w1[j].at[h, 1], am)

    def rs3(j, h):
        (a, ap, am), (b, bp, bm) = first[h], second[h]
        for d, rel, to in ((0, 1, ap), (1, 3, am)):
            rs_landed(j, h, 6 + d, w1[j].at[h, d])
            ref = o(j, h, plus(a, rel), b)
            ref[pl.ds(48 * d, 48), :] += w1[j][h, d]
            rs_send(j, h, 8 + d, ref, w2[j].at[h, d], to)

    def rs4(j, h):
        (a, ap, am), (b, bp, bm) = first[h], second[h]
        for d in range(2):
            rs_landed(j, h, 8 + d, w2[j].at[h, d])
        out[:, columns(j, h)] = o(j, h, a, b)[...] + (w2[j][h, 0] + w2[j][h, 1])
        for key in [k for k in sends if k[1:3] == (j, h)]:
            sent(key)

    steps = dict(
        hop=hop, prepare=prepare, exchange=exchange, take=take, ag0=ag0, agx=agx, ag1=ag1, ag2=ag2, ag3=ag3, ag4=ag4,
        product1=product1, sum1=sum1, sum2=sum2, sum3=sum3, product2=product2, rs0=rs0, rs1=rs1, rs2=rs2, rs3=rs3, rs4=rs4,
    )
    for name, *where in ORDER:
        steps[name](*where)
    for key in list(sends):
        sent(key)


def per_device(old_basis, updated_eigen_matrix, moment):
    dma = pltpu.SemaphoreType.DMA
    shapes = ((2, 4, 4, PART), (ROWS,), (192,), (192,), (192,), (2, 2, 192), (3, 4, PART), (2, 48), (2, PART))
    return pl.pallas_call(
        kernel,
        out_shape=jax.ShapeDtypeStruct((PART, SLAB), F32),
        in_specs=[pl.BlockSpec(memory_space=pl.ANY)] * 3,
        out_specs=pl.BlockSpec(memory_space=pltpu.VMEM),
        scratch_shapes=[pltpu.VMEM((2, *shape, w), F32) for shape in shapes for w in WIDTHS] + [
            pltpu.VMEM((2 * ROWS, DEPTH), BF16),
            pltpu.VMEM((4, 768, 768), BF16),
            pltpu.VMEM((4, ROWS, 384), F32),
            pltpu.VMEM((2, ROWS, 768), F32),
            pltpu.VMEM((2, 768, 256), BF16),
            dma((NCH, 2, 10)), dma((NCH, 2, 10)), dma((NCH, 2, 10)), dma((NCH, 2, 10)),
            dma((NCH, 2, 5)), dma((NCH, 2, 5)), dma((NCH, 2)), dma((NCH, 2)), dma((NCH, 2)), dma((4,)), dma((4,)), dma((2,)),
        ],
        compiler_params=pltpu.CompilerParams(collective_id=0, has_side_effects=True, vmem_limit_bytes=63 * 2**20),
        cost_estimate=pl.CostEstimate(flops=21_700_000_000, bytes_accessed=10_000_000, transcendentals=0),
        name="rebase",
    )(old_basis, updated_eigen_matrix, moment)


def solution(mesh):
    placed = (P("row", "col"), P("row", "col"), P(("col", "row"), None))
    return jax.shard_map(
        per_device, mesh=mesh, in_specs=placed, out_specs=P(("col", "row"), None), check_vma=False
    )
```

```python
import jax
import jax.numpy as jnp
from jax import lax
from jax.experimental import pallas as pl
from jax.experimental.pallas import tpu as pltpu
from jax.sharding import PartitionSpec as P

ROWS, DEPTH, SLAB, PART = 384, 3072, 1536, 96
PLANE = DEPTH // 2
WIDTHS = (256, 128, 128, 128, 128)
NCH = len(WIDTHS)
FROM = [2 * sum(WIDTHS[:j]) for j in range(NCH)]
ORDER = (
    ("hop", 0), ("ag0", 0, 1), ("ag0", 1, 1), ("ag0", 0, 0), ("ag0", 1, 0), ("ag0", 2, 0), ("prepare", 0),
    ("prepare", 1), ("prepare", 2), ("prepare", 3), ("agx", 0, 1), ("hop", 1), ("hop", 2), ("agx", 0, 0), ("hop", 3),
    ("hop", 4), ("ag0", 2, 1), ("ag0", 3, 1), ("ag0", 3, 0), ("prepare", 4), ("prepare", 5), ("agx", 1, 0),
    ("ag1", 0, 1), ("agx", 1, 1), ("ag1", 0, 0), ("agx", 2, 0), ("agx", 2, 1), ("ag1", 1, 0), ("agx", 3, 0),
    ("ag2", 0, 1), ("ag0", 4, 1), ("agx", 3, 1), ("ag2", 0, 0), ("ag0", 4, 0), ("ag1", 1, 1), ("exchange", 0),
    ("exchange", 1), ("exchange", 2), ("exchange", 3), ("ag1", 2, 0), ("ag1", 2, 1), ("agx", 4, 0), ("agx", 4, 1),
    ("ag2", 1, 0), ("ag1", 3, 0), ("ag1", 3, 1), ("ag3", 0, 1), ("ag3", 0, 0), ("ag2", 1, 1), ("ag2", 2, 0),
    ("ag2", 2, 1), ("ag1", 4, 0), ("ag1", 4, 1), ("ag2", 3, 0), ("ag3", 1, 0), ("ag4", 0, 1), ("product1", 0, 1),
    ("ag2", 3, 1), ("sum1", 0, 1), ("ag3", 1, 1), ("ag4", 0, 0), ("product1", 0, 0), ("sum1", 0, 0), ("ag3", 2, 1),
    ("ag3", 2, 0), ("ag2", 4, 0), ("ag2", 4, 1), ("take", 0), ("take", 1), ("take", 2), ("take", 3), ("sum2", 0, 1),
    ("ag3", 3, 1), ("ag3", 3, 0), ("sum2", 0, 0), ("ag4", 1, 1), ("ag4", 1, 0), ("product1", 1, 0), ("sum3", 0, 1),
    ("ag4", 2, 1), ("ag4", 2, 0), ("product1", 2, 0), ("sum3", 0, 0), ("sum1", 1, 0), ("product2", 0, 1),
    ("sum1", 2, 0), ("product2", 0, 0), ("ag3", 4, 1), ("ag3", 4, 0), ("rs0", 0, 1), ("rs0", 0, 0), ("sum2", 1, 0),
    ("ag4", 3, 1), ("ag4", 3, 0), ("product1", 3, 0), ("sum2", 2, 0), ("ag4", 4, 1), ("ag4", 4, 0), ("sum1", 3, 0),
    ("product1", 4, 0), ("sum3", 1, 0), ("rs1", 0, 1), ("rs1", 0, 0), ("sum1", 4, 0), ("product2", 1, 0), ("rs0", 1, 0),
    ("sum3", 2, 0), ("rs0", 1, 1), ("sum2", 3, 0), ("product2", 2, 0), ("rs0", 2, 1), ("rs2", 0, 0), ("rs2", 0, 1),
    ("sum2", 4, 0), ("rs0", 2, 0), ("rs1", 1, 0), ("rs1", 1, 1), ("sum3", 3, 0), ("rs3", 0, 1), ("rs1", 2, 1),
    ("product2", 3, 0), ("sum3", 4, 0), ("rs0", 3, 1), ("rs3", 0, 0), ("rs0", 3, 0), ("rs1", 2, 0), ("product2", 4, 0),
    ("rs0", 4, 0), ("rs0", 4, 1), ("rs2", 2, 1), ("rs4", 0, 1), ("rs1", 3, 1), ("rs1", 3, 0), ("rs2", 1, 1),
    ("rs2", 1, 0), ("rs4", 0, 0), ("rs2", 2, 0), ("rs1", 4, 1), ("rs1", 4, 0), ("rs3", 2, 1), ("rs2", 3, 1),
    ("rs3", 1, 0), ("rs2", 3, 0), ("rs3", 2, 0), ("rs3", 1, 1), ("rs2", 4, 1), ("rs2", 4, 0), ("rs4", 1, 0),
    ("rs4", 2, 1), ("rs3", 3, 0), ("rs3", 3, 1), ("rs4", 2, 0), ("rs4", 1, 1), ("rs3", 4, 0), ("rs3", 4, 1),
    ("rs4", 3, 0), ("rs4", 3, 1), ("rs4", 4, 0), ("rs4", 4, 1),
)
MESH = pl.DeviceIdType.MESH
F32, BF16 = jnp.float32, jnp.bfloat16


def split(v):
    hi = v.astype(BF16)
    return hi, (v - hi.astype(F32)).astype(BF16)


def kernel(q_hbm, u_hbm, m_hbm, out, *scratch):
    per_chunk, common = scratch[: 9 * NCH], scratch[9 * NCH :]
    mg, prod, rd, y1, rf, sf, v, w1, w2 = [per_chunk[i * NCH : (i + 1) * NCH] for i in range(9)]
    qs, uts, urecv, stage, shl, ag_s, ag_r, rs_s, rs_r, ar_s, ar_r, pre_s, pre_r, own_sem, u_s, u_r, st_sem = common
    row, col = lax.axis_index("row"), lax.axis_index("col")
    ylo, x, z = row // 16, lax.rem(row // 4, 4), lax.rem(row, 4)
    yhi, core = col // 2, lax.rem(col, 2)

    def plus(v, n):
        return lax.rem(v + n, 4)

    def in_plane(xx, zz):
        return (ylo * 16 + xx * 4 + zz, col)

    xp, xm = in_plane(plus(x, 1), z), in_plane(plus(x, 3), z)
    zp, zm = in_plane(x, plus(z, 1)), in_plane(x, plus(z, 3))
    pair = ((1 - ylo) * 16 + x * 4 + z, col)
    far = (row, (1 - yhi) * 2 + core)
    sib = (row, yhi * 2 + 1 - core)

    first = ((x, xp, xm), (z, zp, zm))
    second = ((z, zp, zm), (x, xp, xm))

    def remote(src, dst, ss, rs, to):
        return pltpu.make_async_remote_copy(src_ref=src, dst_ref=dst, send_sem=ss, recv_sem=rs, device_id=to, device_id_type=MESH)

    sends = {}

    pairs = {"ag": (ag_s, ag_r), "rs": (rs_s, rs_r), "ar": (ar_s, ar_r), "pre": (pre_s, pre_r), "u": (u_s, u_r)}

    def copy(key, src, dst, to):
        ss, rs = (sem.at[key[1:]] for sem in pairs[key[0]])
        return remote(src, dst, ss, rs, to)

    def send(key, src, dst, to):
        sends[key] = lambda: copy(key, src, dst, to)
        sends[key]().start()

    def landed(key, dst):
        copy(key, dst, dst, pair).wait_recv()

    def sent(key):
        sends.pop(key)().wait_send()

    def columns(j, h):
        return pl.ds(FROM[j] + h * WIDTHS[j], WIDTHS[j])

    def own_piece(j, h, part):
        return mg[j].at[h, part, z, x] if h == 0 else mg[j].at[h, part, x, z]

    def own_copy(j, h):
        return pltpu.make_async_copy(m_hbm.at[:, columns(j, h)], own_piece(j, h, ylo), own_sem.at[j, h])

    def hop(j):
        for h in range(2):
            send(("pre", j, h), m_hbm.at[:, columns(j, h)], own_piece(j, h, ylo), pair)

    def exchange(i):
        at = pl.multiple_of((1 - ylo) * PLANE + 384 * i, 128)
        send(("u", i), u_hbm.at[:, pl.ds(at, 384)], urecv.at[i], pair)

    def load(i):
        if i < 4:
            src = q_hbm.at[:, pl.ds(i * 768, 768)]
        else:
            src = u_hbm.at[:, pl.ds(pl.multiple_of(ylo * PLANE + (i - 4) * 768, 128), 768)]
        return pltpu.make_async_copy(src, stage.at[i % 2], st_sem.at[i % 2])

    def turn(src, seg, depth0):
        @pl.loop(0, 3)
        def _(i):
            at = pl.multiple_of(i * 128, 128)
            hi, lo = split(src[:, pl.ds(at, 128)].T)
            uts[seg, pl.ds(at, 128), pl.ds(depth0, 384)] = hi
            uts[seg, pl.ds(at + 384, 128), pl.ds(depth0, 384)] = lo

    def prepare(i):
        load(i).wait()
        if i < 4:
            @pl.loop(0, 12)
            def _(r):
                r0 = pl.multiple_of(r * 32, 32)
                hi, lo = split(stage[i % 2, pl.ds(r0, 32), :])
                qs[pl.ds(r0, 32), pl.ds(i * 768, 768)] = hi
                qs[pl.ds(r0 + 384, 32), pl.ds(i * 768, 768)] = lo
        else:
            for half in range(2):
                turn(stage.at[i % 2, :, pl.ds(384 * half, 384)], 2 * (i - 4) + half, pl.multiple_of(ylo * 384, 128))
        if i + 2 < 6:
            load(i + 2).start()

    for j in range(NCH):
        for h in range(2):
            own_copy(j, h).start()
    load(0).start()
    load(1).start()

    barrier = pltpu.get_barrier_semaphore()
    for other in (xp, xm, zp, zm, pair, far, sib):
        pl.semaphore_signal(barrier, inc=1, device_id=other, device_id_type=MESH)
    pl.semaphore_wait(barrier, 7)

    def take(i):
        landed(("u", i), urecv.at[i])
        turn(urecv.at[i], i, pl.multiple_of((1 - ylo) * 384, 128))

    def piece(j, h, a, b):
        return mg[j].at[h, :, b, a]

    def line(j, h, part, b):
        return mg[j].at[h, part, b]

    def lines(j, h, b):
        return mg[j].at[h, :, b]

    def half_piece(j, h, part, a, b):
        return mg[j].at[h, part, b, a]

    def pass_on(j, h, i, ref, to):
        send(("ag", j, h, i), ref, ref, to)

    def arrived(j, h, i, ref):
        landed(("ag", j, h, i), ref)

    def ag0(j, h):
        (a, ap, am), (b, bp, bm) = first[h], second[h]
        own_copy(j, h).wait()
        pass_on(j, h, 0, half_piece(j, h, ylo, a, b), ap)
        pass_on(j, h, 1, half_piece(j, h, ylo, a, b), am)

    def agx(j, h):
        (a, ap, am), (b, bp, bm) = first[h], second[h]
        landed(("pre", j, h), own_piece(j, h, 1 - ylo))
        pass_on(j, h, 8, half_piece(j, h, 1 - ylo, a, b), ap)
        pass_on(j, h, 9, half_piece(j, h, 1 - ylo, a, b), am)

    def ag1(j, h):
        (a, ap, am), (b, bp, bm) = first[h], second[h]
        for i, rel, to in ((0, 3, ap), (1, 1, am)):
            arrived(j, h, i, half_piece(j, h, ylo, plus(a, rel), b))
            arrived(j, h, 8 + i, half_piece(j, h, 1 - ylo, plus(a, rel), b))
            pass_on(j, h, 2 + i, half_piece(j, h, i, plus(a, rel), b), to)

    def ag2(j, h):
        (a, ap, am), (b, bp, bm) = first[h], second[h]
        for i in range(2):
            arrived(j, h, 2 + i, half_piece(j, h, i, plus(a, 2), b))
        pass_on(j, h, 4, lines(j, h, b), bp)
        pass_on(j, h, 5, lines(j, h, b), bm)

    def ag3(j, h):
        (a, ap, am), (b, bp, bm) = first[h], second[h]
        for i, rel, to in ((0, 3, bp), (1, 1, bm)):
            arrived(j, h, 4 + i, lines(j, h, plus(b, rel)))
            pass_on(j, h, 6 + i, line(j, h, i, plus(b, rel)), to)

    def ag4(j, h):
        (a, ap, am), (b, bp, bm) = first[h], second[h]
        for i in range(2):
            arrived(j, h, 6 + i, line(j, h, i, plus(b, 2)))

    def halves(j, g):
        return ((0, 1), pl.ds(0, 2)) if WIDTHS[j] < 256 else ((g,), pl.ds(g, 1))

    def ar_send(j, g, i, src, dst, to):
        send(("ar", j, g, i), src, dst, to)

    def ar_landed(j, g, i, dst):
        landed(("ar", j, g, i), dst)

    def moment_rows(j, h, part, x0):
        if h == 0:
            return jnp.concatenate([mg[j][0, part, zz, x0 + xx] for xx in range(2) for zz in range(4)], axis=0)
        return mg[j][1, part, pl.ds(x0, 2)].reshape(768, WIDTHS[j])

    def product1(j, g):
        hs, sl = halves(j, g)
        w = WIDTHS[j]
        prod[j][sl] = jnp.zeros((len(hs), ROWS, w), F32)

        @pl.loop(0, 4)
        def _(i):
            rows = [moment_rows(j, h, i // 2, lax.rem(i, 2) * 2) for h in hs]
            hi, lo = split(jnp.concatenate(rows, axis=1) if len(hs) > 1 else rows[0])
            at = pl.ds(pl.multiple_of(i * 768, 128), 768)
            both = jnp.dot(qs[:, at], hi, preferred_element_type=F32)
            rest = jnp.dot(qs[pl.ds(0, 384), at], lo, preferred_element_type=F32)
            total = both[:ROWS] + (both[ROWS:] + rest)
            for n, h in enumerate(hs):
                prod[j][h] += total[:, n * w : (n + 1) * w]

        ar_send(j, g, 0, prod[j].at[sl, pl.ds(pl.multiple_of((1 - core) * 192, 192), 192)], rd[j].at[sl], sib)

    def sum1(j, g):
        hs, sl = halves(j, g)
        ar_landed(j, g, 0, rd[j].at[sl])
        y1[j][sl] = prod[j][sl, pl.ds(pl.multiple_of(core * 192, 192), 192), :] + rd[j][sl]
        ar_send(j, g, 1, y1[j].at[sl], rf[j].at[sl], far)

    def sum2(j, g):
        hs, sl = halves(j, g)
        ar_landed(j, g, 1, rf[j].at[sl])
        sf[j][sl, ylo, core] = y1[j][sl] + rf[j][sl]
        ref = sf[j].at[sl, ylo, core]
        ar_send(j, g, 2, ref, ref, pair)
        ar_send(j, g, 3, ref, ref, sib)

    def sum3(j, g):
        hs, sl = halves(j, g)
        ref = sf[j].at[sl, 1 - ylo, core]
        ar_landed(j, g, 2, ref)
        ar_send(j, g, 4, ref, ref, sib)

    def product2(j, g):
        hs, sl = halves(j, g)
        w = WIDTHS[j]
        ar_landed(j, g, 3, sf[j].at[sl, ylo, 1 - core])
        ar_landed(j, g, 4, sf[j].at[sl, 1 - ylo, 1 - core])
        for h in hs:
            for i in range(10):
                sent(("ag", j, h, i))

        @pl.loop(0, 4)
        def _(i):
            at = pl.ds(pl.multiple_of(i * 192, 192), 192)
            for n, h in enumerate(hs):
                hi, lo = split(sf[j][h, i // 2, lax.rem(i, 2)])
                shl[0, at, pl.ds(n * w, w)] = hi
                shl[1, at, pl.ds(n * w, w)] = lo

        @pl.loop(0, 4)
        def _(seg):
            both = jnp.dot(uts[seg], shl[0, :, pl.ds(0, len(hs) * w)], preferred_element_type=F32)
            rest = jnp.dot(uts[seg, pl.ds(0, 384), :], shl[1, :, pl.ds(0, len(hs) * w)], preferred_element_type=F32)
            total = both[:384] + (both[384:] + rest)
            for n, h in enumerate(hs):
                blocks = total[:, n * w : (n + 1) * w].reshape(4, PART, w)
                if h == 0:
                    mg[j][0, 0, :, seg] = blocks
                else:
                    mg[j][1, 0, seg] = blocks

    def o(j, h, a, b):
        return mg[j].at[h, 0, b, a]

    def half(k):
        return pl.ds(2 * k, 2)

    def o_half(j, h, k, b):
        return mg[j].at[h, 0, b, half(k)]

    def rs_send(j, h, i, src, dst, to):
        send(("rs", j, h, i), src, dst, to)

    def rs_landed(j, h, i, dst):
        landed(("rs", j, h, i), dst)

    def rs0(j, h):
        (a, ap, am), (b, bp, bm) = first[h], second[h]
        rs_send(j, h, 0, o_half(j, h, 0, plus(b, 2)), v[j].at[h, 0, half(0)], bp)
        rs_send(j, h, 1, o_half(j, h, 1, plus(b, 2)), v[j].at[h, 0, half(1)], bm)
        rs_send(j, h, 2, o_half(j, h, 1, plus(b, 1)), v[j].at[h, 1, half(1)], bp)
        rs_send(j, h, 3, o_half(j, h, 0, plus(b, 3)), v[j].at[h, 2, half(0)], bm)

    def rs1(j, h):
        (a, ap, am), (b, bp, bm) = first[h], second[h]
        for k, bb, to in ((0, plus(b, 1), bp), (1, plus(b, 3), bm)):
            rs_landed(j, h, k, v[j].at[h, 0, half(k)])
            ref = o_half(j, h, k, bb)
            ref[...] += v[j][h, 0, half(k)]
            rs_send(j, h, 4 + k, ref, v[j].at[h, 1 + k, half(k)], to)

    def rs2(j, h):
        (a, ap, am), (b, bp, bm) = first[h], second[h]
        rs_landed(j, h, 2, v[j].at[h, 1, half(1)])
        rs_landed(j, h, 3, v[j].at[h, 2, half(0)])
        rs_landed(j, h, 4, v[j].at[h, 1, half(0)])
        rs_landed(j, h, 5, v[j].at[h, 2, half(1)])
        ref = mg[j].at[h, 0, b]
        ref[...] += v[j][h, 1] + v[j][h, 2]
        far_block = o(j, h, plus(a, 2), b)
        rs_send(j, h, 6, far_block.at[pl.ds(0, 48)], w1[j].at[h, 0], ap)
        rs_send(j, h, 7, far_block.at[pl.ds(48, 48)], w1[j].at[h, 1], am)

    def rs3(j, h):
        (a, ap, am), (b, bp, bm) = first[h], second[h]
        for d, rel, to in ((0, 1, ap), (1, 3, am)):
            rs_landed(j, h, 6 + d, w1[j].at[h, d])
            ref = o(j, h, plus(a, rel), b)
            ref[pl.ds(48 * d, 48), :] += w1[j][h, d]
            rs_send(j, h, 8 + d, ref, w2[j].at[h, d], to)

    def rs4(j, h):
        (a, ap, am), (b, bp, bm) = first[h], second[h]
        for d in range(2):
            rs_landed(j, h, 8 + d, w2[j].at[h, d])
        out[:, columns(j, h)] = o(j, h, a, b)[...] + (w2[j][h, 0] + w2[j][h, 1])
        for key in [k for k in sends if k[1:3] == (j, h)]:
            sent(key)

    steps = dict(
        hop=hop, prepare=prepare, exchange=exchange, take=take, ag0=ag0, agx=agx, ag1=ag1, ag2=ag2, ag3=ag3, ag4=ag4,
        product1=product1, sum1=sum1, sum2=sum2, sum3=sum3, product2=product2, rs0=rs0, rs1=rs1, rs2=rs2, rs3=rs3, rs4=rs4,
    )
    for name, *where in ORDER:
        steps[name](*where)
    for key in list(sends):
        sent(key)


def per_device(old_basis, updated_eigen_matrix, moment):
    dma = pltpu.SemaphoreType.DMA
    shapes = ((2, 4, 4, PART), (ROWS,), (192,), (192,), (192,), (2, 2, 192), (3, 4, PART), (2, 48), (2, PART))
    return pl.pallas_call(
        kernel,
        out_shape=jax.ShapeDtypeStruct((PART, SLAB), F32),
        in_specs=[pl.BlockSpec(memory_space=pl.ANY)] * 3,
        out_specs=pl.BlockSpec(memory_space=pltpu.VMEM),
        scratch_shapes=[pltpu.VMEM((2, *shape, w), F32) for shape in shapes for w in WIDTHS] + [
            pltpu.VMEM((2 * ROWS, DEPTH), BF16),
            pltpu.VMEM((4, 768, 768), BF16),
            pltpu.VMEM((4, ROWS, 384), F32),
            pltpu.VMEM((2, ROWS, 768), F32),
            pltpu.VMEM((2, 768, 256), BF16),
            dma((NCH, 2, 10)), dma((NCH, 2, 10)), dma((NCH, 2, 10)), dma((NCH, 2, 10)),
            dma((NCH, 2, 5)), dma((NCH, 2, 5)), dma((NCH, 2)), dma((NCH, 2)), dma((NCH, 2)), dma((4,)), dma((4,)), dma((2,)),
        ],
        compiler_params=pltpu.CompilerParams(collective_id=0, has_side_effects=True, vmem_limit_bytes=63 * 2**20),
        cost_estimate=pl.CostEstimate(flops=21_700_000_000, bytes_accessed=10_000_000, transcendentals=0),
        name="rebase",
    )(old_basis, updated_eigen_matrix, moment)


def solution(mesh):
    placed = (P("row", "col"), P("row", "col"), P(("col", "row"), None))
    return jax.shard_map(
        per_device, mesh=mesh, in_specs=placed, out_specs=P(("col", "row"), None), check_vma=False
    )
```

```python
import jax
import jax.numpy as jnp
from jax import lax
from jax.experimental import pallas as pl
from jax.experimental.pallas import tpu as pltpu
from jax.sharding import PartitionSpec as P

ROWS, DEPTH, SLAB, PART = 384, 3072, 1536, 96
PLANE = DEPTH // 2
WIDTHS = (256, 128, 128, 128, 128)
NCH = len(WIDTHS)
FROM = [2 * sum(WIDTHS[:j]) for j in range(NCH)]
ORDER = (
    ("hop", 0), ("ag0", 0, 0), ("ag0", 0, 1), ("ag0", 1, 0), ("ag0", 1, 1), ("ag0", 2, 1), ("agx", 0, 0), ("ag0", 2, 0),
    ("agx", 0, 1), ("hop", 1), ("ag0", 3, 0), ("ag0", 3, 1), ("ag0", 4, 0), ("hop", 2), ("ag1", 0, 0), ("hop", 3),
    ("hop", 4), ("ag0", 4, 1), ("ag1", 0, 1), ("agx", 1, 0), ("agx", 2, 0), ("agx", 1, 1), ("exchange", 0),
    ("agx", 2, 1), ("agx", 3, 0), ("ag2", 0, 0), ("ag1", 1, 0), ("agx", 4, 0), ("ag2", 0, 1), ("prepare", 0),
    ("prepare", 1), ("prepare", 2), ("prepare", 3), ("ag1", 2, 1), ("ag1", 2, 0), ("ag1", 1, 1), ("agx", 3, 1),
    ("agx", 4, 1), ("exchange", 1), ("ag3", 0, 0), ("ag1", 3, 0), ("exchange", 2), ("ag1", 4, 0), ("ag3", 0, 1),
    ("ag2", 1, 0), ("exchange", 3), ("ag1", 3, 1), ("ag2", 1, 1), ("prepare", 4), ("prepare", 5), ("ag4", 0, 1),
    ("ag2", 2, 0), ("product1", 0, 1), ("ag2", 2, 1), ("sum1", 0, 1), ("ag4", 0, 0), ("ag3", 1, 1), ("ag1", 4, 1),
    ("ag3", 1, 0), ("product1", 0, 0), ("sum1", 0, 0), ("ag3", 2, 1), ("ag3", 2, 0), ("ag2", 3, 1), ("ag4", 1, 1),
    ("ag2", 4, 1), ("ag2", 3, 0), ("ag4", 1, 0), ("ag2", 4, 0), ("take", 0), ("take", 1), ("take", 2), ("take", 3),
    ("sum2", 0, 1), ("ag4", 2, 1), ("product1", 1, 0), ("sum2", 0, 0), ("ag4", 2, 0), ("product1", 2, 0),
    ("sum3", 0, 1), ("sum1", 1, 0), ("ag3", 3, 0), ("ag3", 3, 1), ("sum1", 2, 0), ("sum3", 0, 0), ("product2", 0, 1),
    ("product2", 0, 0), ("ag3", 4, 1), ("sum2", 1, 0), ("ag3", 4, 0), ("rs0", 0, 1), ("sum2", 2, 0), ("rs0", 0, 0),
    ("ag4", 3, 1), ("ag4", 3, 0), ("product1", 3, 0), ("sum3", 1, 0), ("ag4", 4, 1), ("ag4", 4, 0), ("sum1", 3, 0),
    ("product1", 4, 0), ("sum3", 2, 0), ("rs1", 0, 1), ("rs1", 0, 0), ("sum1", 4, 0), ("product2", 1, 0),
    ("sum2", 3, 0), ("rs0", 1, 1), ("rs0", 1, 0), ("product2", 2, 0), ("rs0", 2, 1), ("sum2", 4, 0), ("rs0", 2, 0),
    ("rs2", 0, 0), ("rs1", 1, 0), ("sum3", 3, 0), ("rs1", 1, 1), ("rs2", 0, 1), ("product2", 3, 0), ("rs0", 3, 1),
    ("rs0", 3, 0), ("sum3", 4, 0), ("rs1", 2, 1), ("rs1", 2, 0), ("product2", 4, 0), ("rs0", 4, 1), ("rs0", 4, 0),
    ("rs1", 3, 1), ("rs1", 3, 0), ("rs1", 4, 1), ("rs2", 1, 0), ("rs1", 4, 0), ("rs2", 2, 0), ("rs2", 2, 1),
    ("rs3", 0, 0), ("rs2", 1, 1), ("rs2", 3, 1), ("rs2", 3, 0), ("rs3", 0, 1), ("rs2", 4, 1), ("rs2", 4, 0),
    ("rs3", 1, 0), ("rs3", 2, 0), ("rs3", 2, 1), ("rs3", 1, 1), ("rs3", 3, 1), ("rs3", 3, 0), ("rs4", 0, 1),
    ("rs3", 4, 0), ("rs3", 4, 1), ("rs4", 0, 0), ("rs4", 2, 1), ("rs4", 2, 0), ("rs4", 1, 0), ("rs4", 3, 0),
    ("rs4", 1, 1), ("rs4", 3, 1), ("rs4", 4, 0), ("rs4", 4, 1),
)
MESH = pl.DeviceIdType.MESH
F32, BF16 = jnp.float32, jnp.bfloat16


def split(v):
    hi = v.astype(BF16)
    return hi, (v - hi.astype(F32)).astype(BF16)


def kernel(q_hbm, u_hbm, m_hbm, out, *scratch):
    per_chunk, common = scratch[: 9 * NCH], scratch[9 * NCH :]
    mg, prod, rd, y1, rf, sf, v, w1, w2 = [per_chunk[i * NCH : (i + 1) * NCH] for i in range(9)]
    qs, uts, urecv, stage, shl, ag_s, ag_r, rs_s, rs_r, ar_s, ar_r, pre_s, pre_r, own_sem, u_s, u_r, st_sem = common
    row, col = lax.axis_index("row"), lax.axis_index("col")
    ylo, x, z = row // 16, lax.rem(row // 4, 4), lax.rem(row, 4)
    yhi, core = col // 2, lax.rem(col, 2)

    def plus(v, n):
        return lax.rem(v + n, 4)

    def in_plane(xx, zz):
        return (ylo * 16 + xx * 4 + zz, col)

    xp, xm = in_plane(plus(x, 1), z), in_plane(plus(x, 3), z)
    zp, zm = in_plane(x, plus(z, 1)), in_plane(x, plus(z, 3))
    pair = ((1 - ylo) * 16 + x * 4 + z, col)
    far = (row, (1 - yhi) * 2 + core)
    sib = (row, yhi * 2 + 1 - core)

    first = ((x, xp, xm), (z, zp, zm))
    second = ((z, zp, zm), (x, xp, xm))

    def remote(src, dst, ss, rs, to):
        return pltpu.make_async_remote_copy(src_ref=src, dst_ref=dst, send_sem=ss, recv_sem=rs, device_id=to, device_id_type=MESH)

    sends = {}

    pairs = {"ag": (ag_s, ag_r), "rs": (rs_s, rs_r), "ar": (ar_s, ar_r), "pre": (pre_s, pre_r), "u": (u_s, u_r)}

    def copy(key, src, dst, to):
        ss, rs = (sem.at[key[1:]] for sem in pairs[key[0]])
        return remote(src, dst, ss, rs, to)

    def send(key, src, dst, to):
        sends[key] = lambda: copy(key, src, dst, to)
        sends[key]().start()

    def landed(key, dst):
        copy(key, dst, dst, pair).wait_recv()

    def sent(key):
        sends.pop(key)().wait_send()

    def columns(j, h):
        return pl.ds(FROM[j] + h * WIDTHS[j], WIDTHS[j])

    def own_piece(j, h, part):
        return mg[j].at[h, part, z, x] if h == 0 else mg[j].at[h, part, x, z]

    def own_copy(j, h):
        return pltpu.make_async_copy(m_hbm.at[:, columns(j, h)], own_piece(j, h, ylo), own_sem.at[j, h])

    def hop(j):
        for h in range(2):
            send(("pre", j, h), m_hbm.at[:, columns(j, h)], own_piece(j, h, ylo), pair)

    def exchange(i):
        at = pl.multiple_of((1 - ylo) * PLANE + 384 * i, 128)
        send(("u", i), u_hbm.at[:, pl.ds(at, 384)], urecv.at[i], pair)

    def load(i):
        if i < 4:
            src = q_hbm.at[:, pl.ds(i * 768, 768)]
        else:
            src = u_hbm.at[:, pl.ds(pl.multiple_of(ylo * PLANE + (i - 4) * 768, 128), 768)]
        return pltpu.make_async_copy(src, stage.at[i % 2], st_sem.at[i % 2])

    def turn(src, seg, depth0):
        @pl.loop(0, 3)
        def _(i):
            at = pl.multiple_of(i * 128, 128)
            hi, lo = split(src[:, pl.ds(at, 128)].T)
            uts[seg, pl.ds(at, 128), pl.ds(depth0, 384)] = hi
            uts[seg, pl.ds(at + 384, 128), pl.ds(depth0, 384)] = lo

    def prepare(i):
        load(i).wait()
        if i < 4:
            @pl.loop(0, 12)
            def _(r):
                r0 = pl.multiple_of(r * 32, 32)
                hi, lo = split(stage[i % 2, pl.ds(r0, 32), :])
                qs[pl.ds(r0, 32), pl.ds(i * 768, 768)] = hi
                qs[pl.ds(r0 + 384, 32), pl.ds(i * 768, 768)] = lo
        else:
            for half in range(2):
                turn(stage.at[i % 2, :, pl.ds(384 * half, 384)], 2 * (i - 4) + half, pl.multiple_of(ylo * 384, 128))
        if i + 2 < 6:
            load(i + 2).start()

    for j in range(NCH):
        for h in range(2):
            own_copy(j, h).start()
    load(0).start()
    load(1).start()

    barrier = pltpu.get_barrier_semaphore()
    for other in (xp, xm, zp, zm, pair, far, sib):
        pl.semaphore_signal(barrier, inc=1, device_id=other, device_id_type=MESH)
    pl.semaphore_wait(barrier, 7)

    def take(i):
        landed(("u", i), urecv.at[i])
        turn(urecv.at[i], i, pl.multiple_of((1 - ylo) * 384, 128))

    def piece(j, h, a, b):
        return mg[j].at[h, :, b, a]

    def line(j, h, part, b):
        return mg[j].at[h, part, b]

    def lines(j, h, b):
        return mg[j].at[h, :, b]

    def half_piece(j, h, part, a, b):
        return mg[j].at[h, part, b, a]

    def pass_on(j, h, i, ref, to):
        send(("ag", j, h, i), ref, ref, to)

    def arrived(j, h, i, ref):
        landed(("ag", j, h, i), ref)

    def ag0(j, h):
        (a, ap, am), (b, bp, bm) = first[h], second[h]
        own_copy(j, h).wait()
        pass_on(j, h, 0, half_piece(j, h, ylo, a, b), ap)
        pass_on(j, h, 1, half_piece(j, h, ylo, a, b), am)

    def agx(j, h):
        (a, ap, am), (b, bp, bm) = first[h], second[h]
        landed(("pre", j, h), own_piece(j, h, 1 - ylo))
        pass_on(j, h, 8, half_piece(j, h, 1 - ylo, a, b), ap)
        pass_on(j, h, 9, half_piece(j, h, 1 - ylo, a, b), am)

    def ag1(j, h):
        (a, ap, am), (b, bp, bm) = first[h], second[h]
        for i, rel, to in ((0, 3, ap), (1, 1, am)):
            arrived(j, h, i, half_piece(j, h, ylo, plus(a, rel), b))
            arrived(j, h, 8 + i, half_piece(j, h, 1 - ylo, plus(a, rel), b))
            pass_on(j, h, 2 + i, half_piece(j, h, i, plus(a, rel), b), to)

    def ag2(j, h):
        (a, ap, am), (b, bp, bm) = first[h], second[h]
        for i in range(2):
            arrived(j, h, 2 + i, half_piece(j, h, i, plus(a, 2), b))
        pass_on(j, h, 4, lines(j, h, b), bp)
        pass_on(j, h, 5, lines(j, h, b), bm)

    def ag3(j, h):
        (a, ap, am), (b, bp, bm) = first[h], second[h]
        for i, rel, to in ((0, 3, bp), (1, 1, bm)):
            arrived(j, h, 4 + i, lines(j, h, plus(b, rel)))
            pass_on(j, h, 6 + i, line(j, h, i, plus(b, rel)), to)

    def ag4(j, h):
        (a, ap, am), (b, bp, bm) = first[h], second[h]
        for i in range(2):
            arrived(j, h, 6 + i, line(j, h, i, plus(b, 2)))

    def halves(j, g):
        return ((0, 1), pl.ds(0, 2)) if WIDTHS[j] < 256 else ((g,), pl.ds(g, 1))

    def ar_send(j, g, i, src, dst, to):
        send(("ar", j, g, i), src, dst, to)

    def ar_landed(j, g, i, dst):
        landed(("ar", j, g, i), dst)

    def moment_rows(j, h, part, x0):
        if h == 0:
            return jnp.concatenate([mg[j][0, part, zz, x0 + xx] for xx in range(2) for zz in range(4)], axis=0)
        return mg[j][1, part, pl.ds(x0, 2)].reshape(768, WIDTHS[j])

    def product1(j, g):
        hs, sl = halves(j, g)
        w = WIDTHS[j]
        prod[j][sl] = jnp.zeros((len(hs), ROWS, w), F32)

        @pl.loop(0, 4)
        def _(i):
            rows = [moment_rows(j, h, i // 2, lax.rem(i, 2) * 2) for h in hs]
            hi, lo = split(jnp.concatenate(rows, axis=1) if len(hs) > 1 else rows[0])
            at = pl.ds(pl.multiple_of(i * 768, 128), 768)
            both = jnp.dot(qs[:, at], hi, preferred_element_type=F32)
            rest = jnp.dot(qs[pl.ds(0, 384), at], lo, preferred_element_type=F32)
            total = both[:ROWS] + (both[ROWS:] + rest)
            for n, h in enumerate(hs):
                prod[j][h] += total[:, n * w : (n + 1) * w]

        ar_send(j, g, 0, prod[j].at[sl, pl.ds(pl.multiple_of((1 - core) * 192, 192), 192)], rd[j].at[sl], sib)

    def sum1(j, g):
        hs, sl = halves(j, g)
        ar_landed(j, g, 0, rd[j].at[sl])
        y1[j][sl] = prod[j][sl, pl.ds(pl.multiple_of(core * 192, 192), 192), :] + rd[j][sl]
        ar_send(j, g, 1, y1[j].at[sl], rf[j].at[sl], far)

    def sum2(j, g):
        hs, sl = halves(j, g)
        ar_landed(j, g, 1, rf[j].at[sl])
        sf[j][sl, ylo, core] = y1[j][sl] + rf[j][sl]
        ref = sf[j].at[sl, ylo, core]
        ar_send(j, g, 2, ref, ref, pair)
        ar_send(j, g, 3, ref, ref, sib)

    def sum3(j, g):
        hs, sl = halves(j, g)
        ref = sf[j].at[sl, 1 - ylo, core]
        ar_landed(j, g, 2, ref)
        ar_send(j, g, 4, ref, ref, sib)

    def product2(j, g):
        hs, sl = halves(j, g)
        w = WIDTHS[j]
        ar_landed(j, g, 3, sf[j].at[sl, ylo, 1 - core])
        ar_landed(j, g, 4, sf[j].at[sl, 1 - ylo, 1 - core])
        for h in hs:
            for i in range(10):
                sent(("ag", j, h, i))

        @pl.loop(0, 4)
        def _(i):
            at = pl.ds(pl.multiple_of(i * 192, 192), 192)
            for n, h in enumerate(hs):
                hi, lo = split(sf[j][h, i // 2, lax.rem(i, 2)])
                shl[0, at, pl.ds(n * w, w)] = hi
                shl[1, at, pl.ds(n * w, w)] = lo

        @pl.loop(0, 4)
        def _(seg):
            both = jnp.dot(uts[seg], shl[0, :, pl.ds(0, len(hs) * w)], preferred_element_type=F32)
            rest = jnp.dot(uts[seg, pl.ds(0, 384), :], shl[1, :, pl.ds(0, len(hs) * w)], preferred_element_type=F32)
            total = both[:384] + (both[384:] + rest)
            for n, h in enumerate(hs):
                blocks = total[:, n * w : (n + 1) * w].reshape(4, PART, w)
                if h == 0:
                    mg[j][0, 0, :, seg] = blocks
                else:
                    mg[j][1, 0, seg] = blocks

    def o(j, h, a, b):
        return mg[j].at[h, 0, b, a]

    def half(k):
        return pl.ds(2 * k, 2)

    def o_half(j, h, k, b):
        return mg[j].at[h, 0, b, half(k)]

    def rs_send(j, h, i, src, dst, to):
        send(("rs", j, h, i), src, dst, to)

    def rs_landed(j, h, i, dst):
        landed(("rs", j, h, i), dst)

    def rs0(j, h):
        (a, ap, am), (b, bp, bm) = first[h], second[h]
        rs_send(j, h, 0, o_half(j, h, 0, plus(b, 2)), v[j].at[h, 0, half(0)], bp)
        rs_send(j, h, 1, o_half(j, h, 1, plus(b, 2)), v[j].at[h, 0, half(1)], bm)
        rs_send(j, h, 2, o_half(j, h, 1, plus(b, 1)), v[j].at[h, 1, half(1)], bp)
        rs_send(j, h, 3, o_half(j, h, 0, plus(b, 3)), v[j].at[h, 2, half(0)], bm)

    def rs1(j, h):
        (a, ap, am), (b, bp, bm) = first[h], second[h]
        for k, bb, to in ((0, plus(b, 1), bp), (1, plus(b, 3), bm)):
            rs_landed(j, h, k, v[j].at[h, 0, half(k)])
            ref = o_half(j, h, k, bb)
            ref[...] += v[j][h, 0, half(k)]
            rs_send(j, h, 4 + k, ref, v[j].at[h, 1 + k, half(k)], to)

    def rs2(j, h):
        (a, ap, am), (b, bp, bm) = first[h], second[h]
        rs_landed(j, h, 2, v[j].at[h, 1, half(1)])
        rs_landed(j, h, 3, v[j].at[h, 2, half(0)])
        rs_landed(j, h, 4, v[j].at[h, 1, half(0)])
        rs_landed(j, h, 5, v[j].at[h, 2, half(1)])
        ref = mg[j].at[h, 0, b]
        ref[...] += v[j][h, 1] + v[j][h, 2]
        far_block = o(j, h, plus(a, 2), b)
        rs_send(j, h, 6, far_block.at[pl.ds(0, 48)], w1[j].at[h, 0], ap)
        rs_send(j, h, 7, far_block.at[pl.ds(48, 48)], w1[j].at[h, 1], am)

    def rs3(j, h):
        (a, ap, am), (b, bp, bm) = first[h], second[h]
        for d, rel, to in ((0, 1, ap), (1, 3, am)):
            rs_landed(j, h, 6 + d, w1[j].at[h, d])
            ref = o(j, h, plus(a, rel), b)
            ref[pl.ds(48 * d, 48), :] += w1[j][h, d]
            rs_send(j, h, 8 + d, ref, w2[j].at[h, d], to)

    def rs4(j, h):
        (a, ap, am), (b, bp, bm) = first[h], second[h]
        for d in range(2):
            rs_landed(j, h, 8 + d, w2[j].at[h, d])
        out[:, columns(j, h)] = o(j, h, a, b)[...] + (w2[j][h, 0] + w2[j][h, 1])
        for key in [k for k in sends if k[1:3] == (j, h)]:
            sent(key)

    steps = dict(
        hop=hop, prepare=prepare, exchange=exchange, take=take, ag0=ag0, agx=agx, ag1=ag1, ag2=ag2, ag3=ag3, ag4=ag4,
        product1=product1, sum1=sum1, sum2=sum2, sum3=sum3, product2=product2, rs0=rs0, rs1=rs1, rs2=rs2, rs3=rs3, rs4=rs4,
    )
    for name, *where in ORDER:
        steps[name](*where)
    for key in list(sends):
        sent(key)


def per_device(old_basis, updated_eigen_matrix, moment):
    dma = pltpu.SemaphoreType.DMA
    shapes = ((2, 4, 4, PART), (ROWS,), (192,), (192,), (192,), (2, 2, 192), (3, 4, PART), (2, 48), (2, PART))
    return pl.pallas_call(
        kernel,
        out_shape=jax.ShapeDtypeStruct((PART, SLAB), F32),
        in_specs=[pl.BlockSpec(memory_space=pl.ANY)] * 3,
        out_specs=pl.BlockSpec(memory_space=pltpu.VMEM),
        scratch_shapes=[pltpu.VMEM((2, *shape, w), F32) for shape in shapes for w in WIDTHS] + [
            pltpu.VMEM((2 * ROWS, DEPTH), BF16),
            pltpu.VMEM((4, 768, 768), BF16),
            pltpu.VMEM((4, ROWS, 384), F32),
            pltpu.VMEM((2, ROWS, 768), F32),
            pltpu.VMEM((2, 768, 256), BF16),
            dma((NCH, 2, 10)), dma((NCH, 2, 10)), dma((NCH, 2, 10)), dma((NCH, 2, 10)),
            dma((NCH, 2, 5)), dma((NCH, 2, 5)), dma((NCH, 2)), dma((NCH, 2)), dma((NCH, 2)), dma((4,)), dma((4,)), dma((2,)),
        ],
        compiler_params=pltpu.CompilerParams(collective_id=0, has_side_effects=True, vmem_limit_bytes=63 * 2**20),
        cost_estimate=pl.CostEstimate(flops=21_700_000_000, bytes_accessed=10_000_000, transcendentals=0),
        name="rebase",
    )(old_basis, updated_eigen_matrix, moment)


def solution(mesh):
    placed = (P("row", "col"), P("row", "col"), P(("col", "row"), None))
    return jax.shard_map(
        per_device, mesh=mesh, in_specs=placed, out_specs=P(("col", "row"), None), check_vma=False
    )
```

```python
import jax
import jax.numpy as jnp
from jax import lax
from jax.experimental import pallas as pl
from jax.experimental.pallas import tpu as pltpu
from jax.sharding import PartitionSpec as P

ROWS, DEPTH, SLAB, PART = 384, 3072, 1536, 96
PLANE = DEPTH // 2
WIDTHS = (128, 256, 128, 128, 128)
NCH = len(WIDTHS)
FROM = [2 * sum(WIDTHS[:j]) for j in range(NCH)]
ORDER = (
    ("hop", 0), ("ag0", 0, 0), ("ag0", 0, 1), ("ag0", 1, 0), ("ag0", 1, 1), ("agx", 0, 0), ("ag0", 2, 1), ("ag0", 2, 0),
    ("agx", 0, 1), ("hop", 1), ("hop", 2), ("ag0", 3, 1), ("ag0", 3, 0), ("ag0", 4, 1), ("ag1", 0, 0), ("ag0", 4, 0),
    ("hop", 3), ("ag1", 0, 1), ("hop", 4), ("agx", 1, 0), ("exchange", 0), ("ag2", 0, 0), ("ag2", 0, 1), ("ag1", 1, 0),
    ("exchange", 1), ("agx", 1, 1), ("agx", 3, 1), ("agx", 4, 0), ("agx", 3, 0), ("agx", 4, 1), ("agx", 2, 1),
    ("ag3", 0, 1), ("ag1", 1, 1), ("ag3", 0, 0), ("agx", 2, 0), ("exchange", 2), ("ag2", 1, 0), ("ag2", 1, 1),
    ("prepare", 0), ("prepare", 1), ("prepare", 2), ("prepare", 3), ("ag1", 3, 1), ("ag1", 2, 0), ("ag1", 3, 0),
    ("ag4", 0, 1), ("ag4", 0, 0), ("ag1", 4, 1), ("ag1", 4, 0), ("ag1", 2, 1), ("product1", 0, 0), ("prepare", 4),
    ("prepare", 5), ("sum1", 0, 0), ("ag3", 1, 1), ("exchange", 3), ("ag3", 1, 0), ("ag2", 2, 0), ("ag2", 2, 1),
    ("sum2", 0, 0), ("ag4", 1, 1), ("ag2", 3, 0), ("ag4", 1, 0), ("product1", 1, 1), ("ag2", 3, 1), ("product1", 1, 0),
    ("sum1", 1, 1), ("take", 0), ("take", 1), ("take", 2), ("take", 3), ("ag3", 2, 1), ("ag3", 2, 0), ("sum3", 0, 0),
    ("sum1", 1, 0), ("ag3", 3, 1), ("ag2", 4, 1), ("ag3", 3, 0), ("product2", 0, 0), ("sum2", 1, 1), ("ag4", 2, 0),
    ("ag2", 4, 0), ("ag4", 2, 1), ("product1", 2, 0), ("ag4", 3, 1), ("sum2", 1, 0), ("rs0", 0, 0), ("ag4", 3, 0),
    ("rs0", 0, 1), ("sum1", 2, 0), ("sum3", 1, 1), ("product1", 3, 0), ("product2", 1, 1), ("sum3", 1, 0),
    ("sum1", 3, 0), ("ag3", 4, 1), ("ag3", 4, 0), ("rs0", 1, 1), ("product2", 1, 0), ("sum2", 2, 0), ("rs0", 1, 0),
    ("sum2", 3, 0), ("ag4", 4, 1), ("ag4", 4, 0), ("product1", 4, 0), ("rs1", 0, 0), ("sum3", 2, 0), ("rs1", 1, 1),
    ("sum1", 4, 0), ("rs1", 0, 1), ("rs1", 1, 0), ("product2", 2, 0), ("sum3", 3, 0), ("rs0", 2, 0), ("rs0", 2, 1),
    ("sum2", 4, 0), ("product2", 3, 0), ("rs0", 3, 1), ("rs2", 1, 1), ("rs1", 2, 1), ("rs0", 3, 0), ("sum3", 4, 0),
    ("rs2", 1, 0), ("rs1", 2, 0), ("rs1", 3, 1), ("product2", 4, 0), ("rs0", 4, 0), ("rs0", 4, 1), ("rs1", 3, 0),
    ("rs2", 2, 0), ("rs2", 0, 0), ("rs1", 4, 0), ("rs2", 0, 1), ("rs1", 4, 1), ("rs2", 2, 1), ("rs2", 3, 1),
    ("rs3", 2, 0), ("rs2", 3, 0), ("rs3", 1, 1), ("rs3", 0, 0), ("rs2", 4, 0), ("rs2", 4, 1), ("rs3", 1, 0),
    ("rs3", 2, 1), ("rs3", 3, 0), ("rs3", 3, 1), ("rs4", 0, 0), ("rs3", 0, 1), ("rs4", 1, 1), ("rs3", 4, 0),
    ("rs3", 4, 1), ("rs4", 2, 1), ("rs4", 1, 0), ("rs4", 2, 0), ("rs4", 3, 0), ("rs4", 3, 1), ("rs4", 0, 1),
    ("rs4", 4, 0), ("rs4", 4, 1),
)
MESH = pl.DeviceIdType.MESH
F32, BF16 = jnp.float32, jnp.bfloat16


def split(v):
    hi = v.astype(BF16)
    return hi, (v - hi.astype(F32)).astype(BF16)


def kernel(q_hbm, u_hbm, m_hbm, out, *scratch):
    per_chunk, common = scratch[: 9 * NCH], scratch[9 * NCH :]
    mg, prod, rd, y1, rf, sf, v, w1, w2 = [per_chunk[i * NCH : (i + 1) * NCH] for i in range(9)]
    qs, uts, urecv, stage, shl, ag_s, ag_r, rs_s, rs_r, ar_s, ar_r, pre_s, pre_r, own_sem, u_s, u_r, st_sem = common
    row, col = lax.axis_index("row"), lax.axis_index("col")
    ylo, x, z = row // 16, lax.rem(row // 4, 4), lax.rem(row, 4)
    yhi, core = col // 2, lax.rem(col, 2)

    def plus(v, n):
        return lax.rem(v + n, 4)

    def in_plane(xx, zz):
        return (ylo * 16 + xx * 4 + zz, col)

    xp, xm = in_plane(plus(x, 1), z), in_plane(plus(x, 3), z)
    zp, zm = in_plane(x, plus(z, 1)), in_plane(x, plus(z, 3))
    pair = ((1 - ylo) * 16 + x * 4 + z, col)
    far = (row, (1 - yhi) * 2 + core)
    sib = (row, yhi * 2 + 1 - core)

    first = ((x, xp, xm), (z, zp, zm))
    second = ((z, zp, zm), (x, xp, xm))

    def remote(src, dst, ss, rs, to):
        return pltpu.make_async_remote_copy(src_ref=src, dst_ref=dst, send_sem=ss, recv_sem=rs, device_id=to, device_id_type=MESH)

    sends = {}

    pairs = {"ag": (ag_s, ag_r), "rs": (rs_s, rs_r), "ar": (ar_s, ar_r), "pre": (pre_s, pre_r), "u": (u_s, u_r)}

    def copy(key, src, dst, to):
        ss, rs = (sem.at[key[1:]] for sem in pairs[key[0]])
        return remote(src, dst, ss, rs, to)

    def send(key, src, dst, to):
        sends[key] = lambda: copy(key, src, dst, to)
        sends[key]().start()

    def landed(key, dst):
        copy(key, dst, dst, pair).wait_recv()

    def sent(key):
        sends.pop(key)().wait_send()

    def columns(j, h):
        return pl.ds(FROM[j] + h * WIDTHS[j], WIDTHS[j])

    def own_piece(j, h, part):
        return mg[j].at[h, part, z, x] if h == 0 else mg[j].at[h, part, x, z]

    def own_copy(j, h):
        return pltpu.make_async_copy(m_hbm.at[:, columns(j, h)], own_piece(j, h, ylo), own_sem.at[j, h])

    def hop(j):
        for h in range(2):
            send(("pre", j, h), m_hbm.at[:, columns(j, h)], own_piece(j, h, ylo), pair)

    def exchange(i):
        at = pl.multiple_of((1 - ylo) * PLANE + 384 * i, 128)
        send(("u", i), u_hbm.at[:, pl.ds(at, 384)], urecv.at[i], pair)

    def load(i):
        if i < 4:
            src = q_hbm.at[:, pl.ds(i * 768, 768)]
        else:
            src = u_hbm.at[:, pl.ds(pl.multiple_of(ylo * PLANE + (i - 4) * 768, 128), 768)]
        return pltpu.make_async_copy(src, stage.at[i % 2], st_sem.at[i % 2])

    def turn(src, seg, depth0):
        @pl.loop(0, 3)
        def _(i):
            at = pl.multiple_of(i * 128, 128)
            hi, lo = split(src[:, pl.ds(at, 128)].T)
            uts[seg, pl.ds(at, 128), pl.ds(depth0, 384)] = hi
            uts[seg, pl.ds(at + 384, 128), pl.ds(depth0, 384)] = lo

    def prepare(i):
        load(i).wait()
        if i < 4:
            @pl.loop(0, 12)
            def _(r):
                r0 = pl.multiple_of(r * 32, 32)
                hi, lo = split(stage[i % 2, pl.ds(r0, 32), :])
                qs[pl.ds(r0, 32), pl.ds(i * 768, 768)] = hi
                qs[pl.ds(r0 + 384, 32), pl.ds(i * 768, 768)] = lo
        else:
            for half in range(2):
                turn(stage.at[i % 2, :, pl.ds(384 * half, 384)], 2 * (i - 4) + half, pl.multiple_of(ylo * 384, 128))
        if i + 2 < 6:
            load(i + 2).start()

    for j in range(NCH):
        for h in range(2):
            own_copy(j, h).start()
    load(0).start()
    load(1).start()

    barrier = pltpu.get_barrier_semaphore()
    for other in (xp, xm, zp, zm, pair, far, sib):
        pl.semaphore_signal(barrier, inc=1, device_id=other, device_id_type=MESH)
    pl.semaphore_wait(barrier, 7)

    def take(i):
        landed(("u", i), urecv.at[i])
        turn(urecv.at[i], i, pl.multiple_of((1 - ylo) * 384, 128))

    def piece(j, h, a, b):
        return mg[j].at[h, :, b, a]

    def line(j, h, part, b):
        return mg[j].at[h, part, b]

    def lines(j, h, b):
        return mg[j].at[h, :, b]

    def half_piece(j, h, part, a, b):
        return mg[j].at[h, part, b, a]

    def pass_on(j, h, i, ref, to):
        send(("ag", j, h, i), ref, ref, to)

    def arrived(j, h, i, ref):
        landed(("ag", j, h, i), ref)

    def ag0(j, h):
        (a, ap, am), (b, bp, bm) = first[h], second[h]
        own_copy(j, h).wait()
        pass_on(j, h, 0, half_piece(j, h, ylo, a, b), ap)
        pass_on(j, h, 1, half_piece(j, h, ylo, a, b), am)

    def agx(j, h):
        (a, ap, am), (b, bp, bm) = first[h], second[h]
        landed(("pre", j, h), own_piece(j, h, 1 - ylo))
        pass_on(j, h, 8, half_piece(j, h, 1 - ylo, a, b), ap)
        pass_on(j, h, 9, half_piece(j, h, 1 - ylo, a, b), am)

    def ag1(j, h):
        (a, ap, am), (b, bp, bm) = first[h], second[h]
        for i, rel, to in ((0, 3, ap), (1, 1, am)):
            arrived(j, h, i, half_piece(j, h, ylo, plus(a, rel), b))
            arrived(j, h, 8 + i, half_piece(j, h, 1 - ylo, plus(a, rel), b))
            pass_on(j, h, 2 + i, half_piece(j, h, i, plus(a, rel), b), to)

    def ag2(j, h):
        (a, ap, am), (b, bp, bm) = first[h], second[h]
        for i in range(2):
            arrived(j, h, 2 + i, half_piece(j, h, i, plus(a, 2), b))
        pass_on(j, h, 4, lines(j, h, b), bp)
        pass_on(j, h, 5, lines(j, h, b), bm)

    def ag3(j, h):
        (a, ap, am), (b, bp, bm) = first[h], second[h]
        for i, rel, to in ((0, 3, bp), (1, 1, bm)):
            arrived(j, h, 4 + i, lines(j, h, plus(b, rel)))
            pass_on(j, h, 6 + i, line(j, h, i, plus(b, rel)), to)

    def ag4(j, h):
        (a, ap, am), (b, bp, bm) = first[h], second[h]
        for i in range(2):
            arrived(j, h, 6 + i, line(j, h, i, plus(b, 2)))

    def halves(j, g):
        return ((0, 1), pl.ds(0, 2)) if WIDTHS[j] < 256 else ((g,), pl.ds(g, 1))

    def ar_send(j, g, i, src, dst, to):
        send(("ar", j, g, i), src, dst, to)

    def ar_landed(j, g, i, dst):
        landed(("ar", j, g, i), dst)

    def moment_rows(j, h, part, x0):
        if h == 0:
            return jnp.concatenate([mg[j][0, part, zz, x0 + xx] for xx in range(2) for zz in range(4)], axis=0)
        return mg[j][1, part, pl.ds(x0, 2)].reshape(768, WIDTHS[j])

    def product1(j, g):
        hs, sl = halves(j, g)
        w = WIDTHS[j]
        prod[j][sl] = jnp.zeros((len(hs), ROWS, w), F32)

        @pl.loop(0, 4)
        def _(i):
            rows = [moment_rows(j, h, i // 2, lax.rem(i, 2) * 2) for h in hs]
            hi, lo = split(jnp.concatenate(rows, axis=1) if len(hs) > 1 else rows[0])
            at = pl.ds(pl.multiple_of(i * 768, 128), 768)
            both = jnp.dot(qs[:, at], hi, preferred_element_type=F32)
            rest = jnp.dot(qs[pl.ds(0, 384), at], lo, preferred_element_type=F32)
            total = both[:ROWS] + (both[ROWS:] + rest)
            for n, h in enumerate(hs):
                prod[j][h] += total[:, n * w : (n + 1) * w]

        ar_send(j, g, 0, prod[j].at[sl, pl.ds(pl.multiple_of((1 - core) * 192, 192), 192)], rd[j].at[sl], sib)

    def sum1(j, g):
        hs, sl = halves(j, g)
        ar_landed(j, g, 0, rd[j].at[sl])
        y1[j][sl] = prod[j][sl, pl.ds(pl.multiple_of(core * 192, 192), 192), :] + rd[j][sl]
        ar_send(j, g, 1, y1[j].at[sl], rf[j].at[sl], far)

    def sum2(j, g):
        hs, sl = halves(j, g)
        ar_landed(j, g, 1, rf[j].at[sl])
        sf[j][sl, ylo, core] = y1[j][sl] + rf[j][sl]
        ref = sf[j].at[sl, ylo, core]
        ar_send(j, g, 2, ref, ref, pair)
        ar_send(j, g, 3, ref, ref, sib)

    def sum3(j, g):
        hs, sl = halves(j, g)
        ref = sf[j].at[sl, 1 - ylo, core]
        ar_landed(j, g, 2, ref)
        ar_send(j, g, 4, ref, ref, sib)

    def product2(j, g):
        hs, sl = halves(j, g)
        w = WIDTHS[j]
        ar_landed(j, g, 3, sf[j].at[sl, ylo, 1 - core])
        ar_landed(j, g, 4, sf[j].at[sl, 1 - ylo, 1 - core])
        for h in hs:
            for i in range(10):
                sent(("ag", j, h, i))

        @pl.loop(0, 4)
        def _(i):
            at = pl.ds(pl.multiple_of(i * 192, 192), 192)
            for n, h in enumerate(hs):
                hi, lo = split(sf[j][h, i // 2, lax.rem(i, 2)])
                shl[0, at, pl.ds(n * w, w)] = hi
                shl[1, at, pl.ds(n * w, w)] = lo

        @pl.loop(0, 4)
        def _(seg):
            both = jnp.dot(uts[seg], shl[0, :, pl.ds(0, len(hs) * w)], preferred_element_type=F32)
            rest = jnp.dot(uts[seg, pl.ds(0, 384), :], shl[1, :, pl.ds(0, len(hs) * w)], preferred_element_type=F32)
            total = both[:384] + (both[384:] + rest)
            for n, h in enumerate(hs):
                blocks = total[:, n * w : (n + 1) * w].reshape(4, PART, w)
                if h == 0:
                    mg[j][0, 0, :, seg] = blocks
                else:
                    mg[j][1, 0, seg] = blocks

    def o(j, h, a, b):
        return mg[j].at[h, 0, b, a]

    def half(k):
        return pl.ds(2 * k, 2)

    def o_half(j, h, k, b):
        return mg[j].at[h, 0, b, half(k)]

    def rs_send(j, h, i, src, dst, to):
        send(("rs", j, h, i), src, dst, to)

    def rs_landed(j, h, i, dst):
        landed(("rs", j, h, i), dst)

    def rs0(j, h):
        (a, ap, am), (b, bp, bm) = first[h], second[h]
        rs_send(j, h, 0, o_half(j, h, 0, plus(b, 2)), v[j].at[h, 0, half(0)], bp)
        rs_send(j, h, 1, o_half(j, h, 1, plus(b, 2)), v[j].at[h, 0, half(1)], bm)
        rs_send(j, h, 2, o_half(j, h, 1, plus(b, 1)), v[j].at[h, 1, half(1)], bp)
        rs_send(j, h, 3, o_half(j, h, 0, plus(b, 3)), v[j].at[h, 2, half(0)], bm)

    def rs1(j, h):
        (a, ap, am), (b, bp, bm) = first[h], second[h]
        for k, bb, to in ((0, plus(b, 1), bp), (1, plus(b, 3), bm)):
            rs_landed(j, h, k, v[j].at[h, 0, half(k)])
            ref = o_half(j, h, k, bb)
            ref[...] += v[j][h, 0, half(k)]
            rs_send(j, h, 4 + k, ref, v[j].at[h, 1 + k, half(k)], to)

    def rs2(j, h):
        (a, ap, am), (b, bp, bm) = first[h], second[h]
        rs_landed(j, h, 2, v[j].at[h, 1, half(1)])
        rs_landed(j, h, 3, v[j].at[h, 2, half(0)])
        rs_landed(j, h, 4, v[j].at[h, 1, half(0)])
        rs_landed(j, h, 5, v[j].at[h, 2, half(1)])
        ref = mg[j].at[h, 0, b]
        ref[...] += v[j][h, 1] + v[j][h, 2]
        far_block = o(j, h, plus(a, 2), b)
        rs_send(j, h, 6, far_block.at[pl.ds(0, 48)], w1[j].at[h, 0], ap)
        rs_send(j, h, 7, far_block.at[pl.ds(48, 48)], w1[j].at[h, 1], am)

    def rs3(j, h):
        (a, ap, am), (b, bp, bm) = first[h], second[h]
        for d, rel, to in ((0, 1, ap), (1, 3, am)):
            rs_landed(j, h, 6 + d, w1[j].at[h, d])
            ref = o(j, h, plus(a, rel), b)
            ref[pl.ds(48 * d, 48), :] += w1[j][h, d]
            rs_send(j, h, 8 + d, ref, w2[j].at[h, d], to)

    def rs4(j, h):
        (a, ap, am), (b, bp, bm) = first[h], second[h]
        for d in range(2):
            rs_landed(j, h, 8 + d, w2[j].at[h, d])
        out[:, columns(j, h)] = o(j, h, a, b)[...] + (w2[j][h, 0] + w2[j][h, 1])
        for key in [k for k in sends if k[1:3] == (j, h)]:
            sent(key)

    steps = dict(
        hop=hop, prepare=prepare, exchange=exchange, take=take, ag0=ag0, agx=agx, ag1=ag1, ag2=ag2, ag3=ag3, ag4=ag4,
        product1=product1, sum1=sum1, sum2=sum2, sum3=sum3, product2=product2, rs0=rs0, rs1=rs1, rs2=rs2, rs3=rs3, rs4=rs4,
    )
    for name, *where in ORDER:
        steps[name](*where)
    for key in list(sends):
        sent(key)


def per_device(old_basis, updated_eigen_matrix, moment):
    dma = pltpu.SemaphoreType.DMA
    shapes = ((2, 4, 4, PART), (ROWS,), (192,), (192,), (192,), (2, 2, 192), (3, 4, PART), (2, 48), (2, PART))
    return pl.pallas_call(
        kernel,
        out_shape=jax.ShapeDtypeStruct((PART, SLAB), F32),
        in_specs=[pl.BlockSpec(memory_space=pl.ANY)] * 3,
        out_specs=pl.BlockSpec(memory_space=pltpu.VMEM),
        scratch_shapes=[pltpu.VMEM((2, *shape, w), F32) for shape in shapes for w in WIDTHS] + [
            pltpu.VMEM((2 * ROWS, DEPTH), BF16),
            pltpu.VMEM((4, 768, 768), BF16),
            pltpu.VMEM((4, ROWS, 384), F32),
            pltpu.VMEM((2, ROWS, 768), F32),
            pltpu.VMEM((2, 768, 256), BF16),
            dma((NCH, 2, 10)), dma((NCH, 2, 10)), dma((NCH, 2, 10)), dma((NCH, 2, 10)),
            dma((NCH, 2, 5)), dma((NCH, 2, 5)), dma((NCH, 2)), dma((NCH, 2)), dma((NCH, 2)), dma((4,)), dma((4,)), dma((2,)),
        ],
        compiler_params=pltpu.CompilerParams(collective_id=0, has_side_effects=True, vmem_limit_bytes=63 * 2**20),
        cost_estimate=pl.CostEstimate(flops=21_700_000_000, bytes_accessed=10_000_000, transcendentals=0),
        name="rebase",
    )(old_basis, updated_eigen_matrix, moment)


def solution(mesh):
    placed = (P("row", "col"), P("row", "col"), P(("col", "row"), None))
    return jax.shard_map(
        per_device, mesh=mesh, in_specs=placed, out_specs=P(("col", "row"), None), check_vma=False
    )
```

```python
import jax
import jax.numpy as jnp
from jax import lax
from jax.experimental import pallas as pl
from jax.experimental.pallas import tpu as pltpu
from jax.sharding import PartitionSpec as P

ROWS, DEPTH, SLAB, PART = 384, 3072, 1536, 96
PLANE = DEPTH // 2
WIDTHS = (128, 256, 128, 128, 128)
NCH = len(WIDTHS)
FROM = [2 * sum(WIDTHS[:j]) for j in range(NCH)]
ORDER = (
    ("hop", 0), ("ag0", 0, 0), ("ag0", 0, 1), ("ag0", 1, 0), ("ag0", 1, 1), ("agx", 0, 0), ("ag0", 2, 1), ("ag0", 2, 0),
    ("agx", 0, 1), ("hop", 1), ("hop", 2), ("ag0", 3, 1), ("ag0", 3, 0), ("ag0", 4, 1), ("ag1", 0, 0), ("ag0", 4, 0),
    ("hop", 3), ("ag1", 0, 1), ("hop", 4), ("agx", 1, 0), ("exchange", 0), ("ag2", 0, 0), ("ag2", 0, 1), ("ag1", 1, 0),
    ("exchange", 1), ("agx", 1, 1), ("agx", 3, 1), ("agx", 4, 0), ("agx", 3, 0), ("agx", 4, 1), ("agx", 2, 1),
    ("ag3", 0, 1), ("ag1", 1, 1), ("ag3", 0, 0), ("agx", 2, 0), ("exchange", 2), ("ag2", 1, 0), ("ag2", 1, 1),
    ("prepare", 0), ("prepare", 1), ("prepare", 2), ("prepare", 3), ("ag1", 3, 1), ("ag1", 2, 0), ("ag1", 3, 0),
    ("ag4", 0, 1), ("ag4", 0, 0), ("ag1", 4, 1), ("ag1", 4, 0), ("ag1", 2, 1), ("product1", 0, 0), ("prepare", 4),
    ("prepare", 5), ("sum1", 0, 0), ("ag3", 1, 1), ("exchange", 3), ("ag3", 1, 0), ("ag2", 2, 0), ("ag2", 2, 1),
    ("sum2", 0, 0), ("ag4", 1, 1), ("ag2", 3, 0), ("ag4", 1, 0), ("product1", 1, 1), ("ag2", 3, 1), ("product1", 1, 0),
    ("sum1", 1, 1), ("take", 0), ("take", 1), ("take", 2), ("take", 3), ("ag3", 2, 1), ("ag3", 2, 0), ("sum3", 0, 0),
    ("sum1", 1, 0), ("ag3", 3, 1), ("ag2", 4, 1), ("ag3", 3, 0), ("product2", 0, 0), ("sum2", 1, 1), ("ag4", 2, 0),
    ("ag2", 4, 0), ("ag4", 2, 1), ("product1", 2, 0), ("ag4", 3, 1), ("sum2", 1, 0), ("rs0", 0, 0), ("ag4", 3, 0),
    ("rs0", 0, 1), ("sum1", 2, 0), ("sum3", 1, 1), ("product1", 3, 0), ("product2", 1, 1), ("sum3", 1, 0),
    ("sum1", 3, 0), ("ag3", 4, 1), ("ag3", 4, 0), ("rs0", 1, 1), ("product2", 1, 0), ("sum2", 2, 0), ("rs0", 1, 0),
    ("sum2", 3, 0), ("ag4", 4, 1), ("ag4", 4, 0), ("product1", 4, 0), ("rs1", 0, 0), ("sum3", 2, 0), ("rs1", 1, 1),
    ("sum1", 4, 0), ("rs1", 0, 1), ("rs1", 1, 0), ("product2", 2, 0), ("sum3", 3, 0), ("rs0", 2, 0), ("rs0", 2, 1),
    ("sum2", 4, 0), ("product2", 3, 0), ("rs0", 3, 1), ("rs2", 1, 1), ("rs1", 2, 1), ("rs0", 3, 0), ("sum3", 4, 0),
    ("rs2", 1, 0), ("rs1", 2, 0), ("rs1", 3, 1), ("product2", 4, 0), ("rs0", 4, 0), ("rs0", 4, 1), ("rs1", 3, 0),
    ("rs2", 2, 0), ("rs2", 0, 0), ("rs1", 4, 0), ("rs2", 0, 1), ("rs1", 4, 1), ("rs2", 2, 1), ("rs2", 3, 1),
    ("rs3", 2, 0), ("rs2", 3, 0), ("rs3", 1, 1), ("rs3", 0, 0), ("rs2", 4, 0), ("rs2", 4, 1), ("rs3", 1, 0),
    ("rs3", 2, 1), ("rs3", 3, 0), ("rs3", 3, 1), ("rs4", 0, 0), ("rs3", 0, 1), ("rs4", 1, 1), ("rs3", 4, 0),
    ("rs3", 4, 1), ("rs4", 2, 1), ("rs4", 1, 0), ("rs4", 2, 0), ("rs4", 3, 0), ("rs4", 3, 1), ("rs4", 0, 1),
    ("rs4", 4, 0), ("rs4", 4, 1),
)
MESH = pl.DeviceIdType.MESH
F32, BF16 = jnp.float32, jnp.bfloat16


def split(v):
    hi = v.astype(BF16)
    return hi, (v - hi.astype(F32)).astype(BF16)


def kernel(q_hbm, u_hbm, m_hbm, out, *scratch):
    per_chunk, common = scratch[: 9 * NCH], scratch[9 * NCH :]
    mg, prod, rd, y1, rf, sf, v, w1, w2 = [per_chunk[i * NCH : (i + 1) * NCH] for i in range(9)]
    qs, uts, urecv, stage, shl, ag_s, ag_r, rs_s, rs_r, ar_s, ar_r, pre_s, pre_r, own_sem, u_s, u_r, st_sem = common
    row, col = lax.axis_index("row"), lax.axis_index("col")
    ylo, x, z = row // 16, lax.rem(row // 4, 4), lax.rem(row, 4)
    yhi, core = col // 2, lax.rem(col, 2)

    def plus(v, n):
        return lax.rem(v + n, 4)

    def in_plane(xx, zz):
        return (ylo * 16 + xx * 4 + zz, col)

    xp, xm = in_plane(plus(x, 1), z), in_plane(plus(x, 3), z)
    zp, zm = in_plane(x, plus(z, 1)), in_plane(x, plus(z, 3))
    pair = ((1 - ylo) * 16 + x * 4 + z, col)
    far = (row, (1 - yhi) * 2 + core)
    sib = (row, yhi * 2 + 1 - core)

    first = ((x, xp, xm), (z, zp, zm))
    second = ((z, zp, zm), (x, xp, xm))

    def remote(src, dst, ss, rs, to):
        return pltpu.make_async_remote_copy(src_ref=src, dst_ref=dst, send_sem=ss, recv_sem=rs, device_id=to, device_id_type=MESH)

    sends = {}

    pairs = {"ag": (ag_s, ag_r), "rs": (rs_s, rs_r), "ar": (ar_s, ar_r), "pre": (pre_s, pre_r), "u": (u_s, u_r)}

    def copy(key, src, dst, to):
        ss, rs = (sem.at[key[1:]] for sem in pairs[key[0]])
        return remote(src, dst, ss, rs, to)

    def send(key, src, dst, to):
        sends[key] = lambda: copy(key, src, dst, to)
        sends[key]().start()

    def landed(key, dst):
        copy(key, dst, dst, pair).wait_recv()

    def sent(key):
        sends.pop(key)().wait_send()

    def columns(j, h):
        return pl.ds(FROM[j] + h * WIDTHS[j], WIDTHS[j])

    def own_piece(j, h, part):
        return mg[j].at[h, part, z, x] if h == 0 else mg[j].at[h, part, x, z]

    def own_copy(j, h):
        return pltpu.make_async_copy(m_hbm.at[:, columns(j, h)], own_piece(j, h, ylo), own_sem.at[j, h])

    def hop(j):
        for h in range(2):
            send(("pre", j, h), m_hbm.at[:, columns(j, h)], own_piece(j, h, ylo), pair)

    def exchange(i):
        at = pl.multiple_of((1 - ylo) * PLANE + 384 * i, 128)
        send(("u", i), u_hbm.at[:, pl.ds(at, 384)], urecv.at[i], pair)

    def load(i):
        if i < 4:
            src = q_hbm.at[:, pl.ds(i * 768, 768)]
        else:
            src = u_hbm.at[:, pl.ds(pl.multiple_of(ylo * PLANE + (i - 4) * 768, 128), 768)]
        return pltpu.make_async_copy(src, stage.at[i % 2], st_sem.at[i % 2])

    def turn(src, seg, depth0):
        @pl.loop(0, 3)
        def _(i):
            at = pl.multiple_of(i * 128, 128)
            hi, lo = split(src[:, pl.ds(at, 128)].T)
            uts[seg, pl.ds(at, 128), pl.ds(depth0, 384)] = hi
            uts[seg, pl.ds(at + 384, 128), pl.ds(depth0, 384)] = lo

    def prepare(i):
        load(i).wait()
        if i < 4:
            @pl.loop(0, 12)
            def _(r):
                r0 = pl.multiple_of(r * 32, 32)
                hi, lo = split(stage[i % 2, pl.ds(r0, 32), :])
                qs[pl.ds(r0, 32), pl.ds(i * 768, 768)] = hi
                qs[pl.ds(r0 + 384, 32), pl.ds(i * 768, 768)] = lo
        else:
            for half in range(2):
                turn(stage.at[i % 2, :, pl.ds(384 * half, 384)], 2 * (i - 4) + half, pl.multiple_of(ylo * 384, 128))
        if i + 2 < 6:
            load(i + 2).start()

    for j in range(NCH):
        for h in range(2):
            own_copy(j, h).start()
    load(0).start()
    load(1).start()

    barrier = pltpu.get_barrier_semaphore()
    for other in (xp, xm, zp, zm, pair, far, sib):
        pl.semaphore_signal(barrier, inc=1, device_id=other, device_id_type=MESH)
    pl.semaphore_wait(barrier, 7)

    def take(i):
        landed(("u", i), urecv.at[i])
        turn(urecv.at[i], i, pl.multiple_of((1 - ylo) * 384, 128))

    def piece(j, h, a, b):
        return mg[j].at[h, :, b, a]

    def line(j, h, part, b):
        return mg[j].at[h, part, b]

    def lines(j, h, b):
        return mg[j].at[h, :, b]

    def half_piece(j, h, part, a, b):
        return mg[j].at[h, part, b, a]

    def pass_on(j, h, i, ref, to):
        send(("ag", j, h, i), ref, ref, to)

    def arrived(j, h, i, ref):
        landed(("ag", j, h, i), ref)

    def ag0(j, h):
        (a, ap, am), (b, bp, bm) = first[h], second[h]
        own_copy(j, h).wait()
        pass_on(j, h, 0, half_piece(j, h, ylo, a, b), ap)
        pass_on(j, h, 1, half_piece(j, h, ylo, a, b), am)

    def agx(j, h):
        (a, ap, am), (b, bp, bm) = first[h], second[h]
        landed(("pre", j, h), own_piece(j, h, 1 - ylo))
        pass_on(j, h, 8, half_piece(j, h, 1 - ylo, a, b), ap)
        pass_on(j, h, 9, half_piece(j, h, 1 - ylo, a, b), am)

    def ag1(j, h):
        (a, ap, am), (b, bp, bm) = first[h], second[h]
        for i, rel, to in ((0, 3, ap), (1, 1, am)):
            arrived(j, h, i, half_piece(j, h, ylo, plus(a, rel), b))
            arrived(j, h, 8 + i, half_piece(j, h, 1 - ylo, plus(a, rel), b))
            pass_on(j, h, 2 + i, half_piece(j, h, i, plus(a, rel), b), to)

    def ag2(j, h):
        (a, ap, am), (b, bp, bm) = first[h], second[h]
        for i in range(2):
            arrived(j, h, 2 + i, half_piece(j, h, i, plus(a, 2), b))
        pass_on(j, h, 4, lines(j, h, b), bp)
        pass_on(j, h, 5, lines(j, h, b), bm)

    def ag3(j, h):
        (a, ap, am), (b, bp, bm) = first[h], second[h]
        for i, rel, to in ((0, 3, bp), (1, 1, bm)):
            arrived(j, h, 4 + i, lines(j, h, plus(b, rel)))
            pass_on(j, h, 6 + i, line(j, h, i, plus(b, rel)), to)

    def ag4(j, h):
        (a, ap, am), (b, bp, bm) = first[h], second[h]
        for i in range(2):
            arrived(j, h, 6 + i, line(j, h, i, plus(b, 2)))

    def halves(j, g):
        return ((0, 1), pl.ds(0, 2)) if WIDTHS[j] < 256 else ((g,), pl.ds(g, 1))

    def ar_send(j, g, i, src, dst, to):
        send(("ar", j, g, i), src, dst, to)

    def ar_landed(j, g, i, dst):
        landed(("ar", j, g, i), dst)

    def moment_rows(j, h, part, x0):
        if h == 0:
            return jnp.concatenate([mg[j][0, part, zz, x0 + xx] for xx in range(2) for zz in range(4)], axis=0)
        return mg[j][1, part, pl.ds(x0, 2)].reshape(768, WIDTHS[j])

    def product1(j, g):
        hs, sl = halves(j, g)
        w = WIDTHS[j]
        prod[j][sl] = jnp.zeros((len(hs), ROWS, w), F32)

        @pl.loop(0, 4)
        def _(i):
            rows = [moment_rows(j, h, i // 2, lax.rem(i, 2) * 2) for h in hs]
            hi, lo = split(jnp.concatenate(rows, axis=1) if len(hs) > 1 else rows[0])
            at = pl.ds(pl.multiple_of(i * 768, 128), 768)
            both = jnp.dot(qs[:, at], hi, preferred_element_type=F32)
            rest = jnp.dot(qs[pl.ds(0, 384), at], lo, preferred_element_type=F32)
            total = both[:ROWS] + (both[ROWS:] + rest)
            for n, h in enumerate(hs):
                prod[j][h] += total[:, n * w : (n + 1) * w]

        ar_send(j, g, 0, prod[j].at[sl, pl.ds(pl.multiple_of((1 - core) * 192, 192), 192)], rd[j].at[sl], sib)

    def sum1(j, g):
        hs, sl = halves(j, g)
        ar_landed(j, g, 0, rd[j].at[sl])
        y1[j][sl] = prod[j][sl, pl.ds(pl.multiple_of(core * 192, 192), 192), :] + rd[j][sl]
        ar_send(j, g, 1, y1[j].at[sl], rf[j].at[sl], far)

    def sum2(j, g):
        hs, sl = halves(j, g)
        ar_landed(j, g, 1, rf[j].at[sl])
        sf[j][sl, ylo, core] = y1[j][sl] + rf[j][sl]
        ref = sf[j].at[sl, ylo, core]
        ar_send(j, g, 2, ref, ref, pair)
        ar_send(j, g, 3, ref, ref, sib)

    def sum3(j, g):
        hs, sl = halves(j, g)
        ref = sf[j].at[sl, 1 - ylo, core]
        ar_landed(j, g, 2, ref)
        ar_send(j, g, 4, ref, ref, sib)

    def product2(j, g):
        hs, sl = halves(j, g)
        w = WIDTHS[j]
        ar_landed(j, g, 3, sf[j].at[sl, ylo, 1 - core])
        ar_landed(j, g, 4, sf[j].at[sl, 1 - ylo, 1 - core])
        for h in hs:
            for i in range(10):
                sent(("ag", j, h, i))

        @pl.loop(0, 4, unroll=True)
        def _(i):
            at = pl.ds(pl.multiple_of(i * 192, 192), 192)
            for n, h in enumerate(hs):
                hi, lo = split(sf[j][h, i // 2, lax.rem(i, 2)])
                shl[0, at, pl.ds(n * w, w)] = hi
                shl[1, at, pl.ds(n * w, w)] = lo

        @pl.loop(0, 4, unroll=True)
        def _(seg):
            both = jnp.dot(uts[seg], shl[0, :, pl.ds(0, len(hs) * w)], preferred_element_type=F32)
            rest = jnp.dot(uts[seg, pl.ds(0, 384), :], shl[1, :, pl.ds(0, len(hs) * w)], preferred_element_type=F32)
            total = both[:384] + (both[384:] + rest)
            for n, h in enumerate(hs):
                blocks = total[:, n * w : (n + 1) * w].reshape(4, PART, w)
                if h == 0:
                    mg[j][0, 0, :, seg] = blocks
                else:
                    mg[j][1, 0, seg] = blocks

    def o(j, h, a, b):
        return mg[j].at[h, 0, b, a]

    def half(k):
        return pl.ds(2 * k, 2)

    def o_half(j, h, k, b):
        return mg[j].at[h, 0, b, half(k)]

    def rs_send(j, h, i, src, dst, to):
        send(("rs", j, h, i), src, dst, to)

    def rs_landed(j, h, i, dst):
        landed(("rs", j, h, i), dst)

    def rs0(j, h):
        (a, ap, am), (b, bp, bm) = first[h], second[h]
        rs_send(j, h, 0, o_half(j, h, 0, plus(b, 2)), v[j].at[h, 0, half(0)], bp)
        rs_send(j, h, 1, o_half(j, h, 1, plus(b, 2)), v[j].at[h, 0, half(1)], bm)
        rs_send(j, h, 2, o_half(j, h, 1, plus(b, 1)), v[j].at[h, 1, half(1)], bp)
        rs_send(j, h, 3, o_half(j, h, 0, plus(b, 3)), v[j].at[h, 2, half(0)], bm)

    def rs1(j, h):
        (a, ap, am), (b, bp, bm) = first[h], second[h]
        for k, bb, to in ((0, plus(b, 1), bp), (1, plus(b, 3), bm)):
            rs_landed(j, h, k, v[j].at[h, 0, half(k)])
            ref = o_half(j, h, k, bb)
            ref[...] += v[j][h, 0, half(k)]
            rs_send(j, h, 4 + k, ref, v[j].at[h, 1 + k, half(k)], to)

    def rs2(j, h):
        (a, ap, am), (b, bp, bm) = first[h], second[h]
        rs_landed(j, h, 2, v[j].at[h, 1, half(1)])
        rs_landed(j, h, 3, v[j].at[h, 2, half(0)])
        rs_landed(j, h, 4, v[j].at[h, 1, half(0)])
        rs_landed(j, h, 5, v[j].at[h, 2, half(1)])
        ref = mg[j].at[h, 0, b]
        ref[...] += v[j][h, 1] + v[j][h, 2]
        far_block = o(j, h, plus(a, 2), b)
        rs_send(j, h, 6, far_block.at[pl.ds(0, 48)], w1[j].at[h, 0], ap)
        rs_send(j, h, 7, far_block.at[pl.ds(48, 48)], w1[j].at[h, 1], am)

    def rs3(j, h):
        (a, ap, am), (b, bp, bm) = first[h], second[h]
        for d, rel, to in ((0, 1, ap), (1, 3, am)):
            rs_landed(j, h, 6 + d, w1[j].at[h, d])
            ref = o(j, h, plus(a, rel), b)
            ref[pl.ds(48 * d, 48), :] += w1[j][h, d]
            rs_send(j, h, 8 + d, ref, w2[j].at[h, d], to)

    def rs4(j, h):
        (a, ap, am), (b, bp, bm) = first[h], second[h]
        for d in range(2):
            rs_landed(j, h, 8 + d, w2[j].at[h, d])
        out[:, columns(j, h)] = o(j, h, a, b)[...] + (w2[j][h, 0] + w2[j][h, 1])
        for key in [k for k in sends if k[1:3] == (j, h)]:
            sent(key)

    steps = dict(
        hop=hop, prepare=prepare, exchange=exchange, take=take, ag0=ag0, agx=agx, ag1=ag1, ag2=ag2, ag3=ag3, ag4=ag4,
        product1=product1, sum1=sum1, sum2=sum2, sum3=sum3, product2=product2, rs0=rs0, rs1=rs1, rs2=rs2, rs3=rs3, rs4=rs4,
    )
    for name, *where in ORDER:
        steps[name](*where)
    for key in list(sends):
        sent(key)


def per_device(old_basis, updated_eigen_matrix, moment):
    dma = pltpu.SemaphoreType.DMA
    shapes = ((2, 4, 4, PART), (ROWS,), (192,), (192,), (192,), (2, 2, 192), (3, 4, PART), (2, 48), (2, PART))
    return pl.pallas_call(
        kernel,
        out_shape=jax.ShapeDtypeStruct((PART, SLAB), F32),
        in_specs=[pl.BlockSpec(memory_space=pl.ANY)] * 3,
        out_specs=pl.BlockSpec(memory_space=pltpu.VMEM),
        scratch_shapes=[pltpu.VMEM((2, *shape, w), F32) for shape in shapes for w in WIDTHS] + [
            pltpu.VMEM((2 * ROWS, DEPTH), BF16),
            pltpu.VMEM((4, 768, 768), BF16),
            pltpu.VMEM((4, ROWS, 384), F32),
            pltpu.VMEM((2, ROWS, 768), F32),
            pltpu.VMEM((2, 768, 256), BF16),
            dma((NCH, 2, 10)), dma((NCH, 2, 10)), dma((NCH, 2, 10)), dma((NCH, 2, 10)),
            dma((NCH, 2, 5)), dma((NCH, 2, 5)), dma((NCH, 2)), dma((NCH, 2)), dma((NCH, 2)), dma((4,)), dma((4,)), dma((2,)),
        ],
        compiler_params=pltpu.CompilerParams(collective_id=0, has_side_effects=True, vmem_limit_bytes=63 * 2**20),
        cost_estimate=pl.CostEstimate(flops=21_700_000_000, bytes_accessed=10_000_000, transcendentals=0),
        name="rebase",
    )(old_basis, updated_eigen_matrix, moment)


def solution(mesh):
    placed = (P("row", "col"), P("row", "col"), P(("col", "row"), None))
    return jax.shard_map(
        per_device, mesh=mesh, in_specs=placed, out_specs=P(("col", "row"), None), check_vma=False
    )
```
